32 devices in a mesh: row: 4 (over y, x), col: 8 (over z, core).
Axes of the slice: x: 2, y: 2, z: 4, core: 2. Of those that a mesh axis runs over, the one named last changes fastest.
Arguments:
- observed: float32 [16, 512, 1024], P(None, 'row', 'col'), may hold values from 0.2 to 3
- estimate: float32 [16, 512, 1024], P(None, 'row', 'col'), may hold values from 0.5 to 2
- psf_bank: float32 [128, 16, 2, 4, 33], P(('row', 'col')), may hold values from 0.05 to 1
- zone_ids: int32 [4, 8, 16, 2], P('row', 'col'), may hold values from 0 to 31, all different within a row
- mix_weights: float32 [4, 8, 16, 2], P('row', 'col'), may hold values from 0.2 to 1
- illumination: float32 [16, 64, 8], P(None, 'row', 'col'), may hold values from 0.3 to 3
Outputs:
- restored: float32 [16, 512, 1024], P(None, 'row', 'col')
The draws below stay inside these ranges and needn't reach their ends.
Inputs may be any that keep to these rules, and one draw needn't show every extreme that they name: `zone_ids`: at each depth a tile names 2 different zones.
All inputs are finite; a program needn't handle non-finite values.
Results may differ from the reference program's by a relative error of at most 0.001.
Values may be sent and summed in bfloat16 or wider, within the bound.
No kernel may reach another device: no remote copies, remote signals or barrier semaphores. Data moves between devices by JAX's collectives and lax.ppermute only.
A program may use at most 192 MiB of HBM per device.

```python
import math
import jax
import jax.numpy as jnp
from jax import lax

TR = 128
TC = 128
DEPTH = 16
TAPS = 33
RANK = 4
K = 2
CR = 16
ITERS = 2
NY = 512
NX = 1024
ZBAND = 32
COARSE = 64
N_ROW = 4
N_COL = 8


def block_levels(rng, extent, pieces, smallest, top_value):
    loudness = 1.0
    for position, parts in pieces:
        steps = jax.random.uniform(jax.random.fold_in(jax.random.fold_in(rng, 6), position), (parts,), jnp.float32, smallest / len(pieces), top_value / len(pieces))
        loudness = loudness * jnp.repeat(jnp.exp(steps), extent[position] // parts).reshape((-1,) + (1,) * (len(extent) - 1 - position))
    return loudness


def different_ones(rng, rows, amount, top, lift):
    ranking = jax.random.permutation(jax.random.fold_in(rng, 1), amount)
    pull = ranking
    for power in range(3):
        pull = pull * pull // amount
    pull = pull * lift // amount
    lots = jax.random.randint(jax.random.fold_in(rng, 2), (rows, amount), 0, 4096) + pull
    holders = jax.random.permutation(jax.random.fold_in(rng, 3), rows)[jnp.arange(amount) % rows]
    lots = jnp.where(jnp.arange(rows)[:, None] == holders[None, :], 1 << 14, lots)
    score = lots * amount + jnp.arange(amount)
    return lax.top_k(score.astype(jnp.int32), top)[1].astype(jnp.int32)


def setup_inputs(seed: int = 0) -> dict:
    splits = jax.random.split(jax.random.key(seed), 7)
    return {
        "observed": jnp.clip(0.2 + 2.8 * jax.random.uniform(splits[0], (DEPTH, NY, NX), jnp.float32) ** block_levels(splits[0], (DEPTH, NY, NX), ((1, 4), (2, 8)), -0.2, 0.2), 0.2, 3.0),
        "estimate": jnp.clip(0.5 + 1.5 * jax.random.uniform(splits[1], (DEPTH, NY, NX), jnp.float32) ** block_levels(splits[1], (DEPTH, NY, NX), ((1, 4), (2, 8)), -0.2, 0.2), 0.5, 2.0),
        "psf_bank": jnp.clip(jnp.exp(math.log(1.0) - 2.9957323 * jax.random.uniform(splits[2], (N_ROW * ZBAND, DEPTH, 2, RANK, TAPS), jnp.float32) ** block_levels(splits[2], (N_ROW * ZBAND, DEPTH, 2, RANK, TAPS), ((0, 32),), -0.2, 0.2)), 0.05, 1.0),
        "zone_ids": different_ones(splits[3], N_ROW * N_COL * DEPTH, ZBAND, K, 1024).reshape((N_ROW, N_COL, DEPTH, K)),
        "mix_weights": jnp.clip(jnp.exp(math.log(1.0) - 1.609438 * jax.random.uniform(splits[4], (N_ROW, N_COL, DEPTH, K), jnp.float32) ** block_levels(splits[4], (N_ROW, N_COL, DEPTH, K), ((0, 4), (1, 8)), -0.2, 0.2)), 0.2, 1.0),
        "illumination": jnp.clip(jnp.exp(math.log(3.0) - 2.3025851 * jax.random.uniform(splits[5], (DEPTH, COARSE, N_COL), jnp.float32) ** block_levels(splits[5], (DEPTH, COARSE, N_COL), ((1, 4), (2, 8)), -0.2, 0.2)), 0.3, 3.0),
    }


def band_table(size, taps):
    half = taps // 2
    offsets = jnp.arange(size + 2 * half, dtype=jnp.int32)[None, :] - jnp.arange(size, dtype=jnp.int32)[:, None]
    return (offsets[None, :, :] == jnp.arange(taps, dtype=jnp.int32)[:, None, None]).astype(jnp.float32)

def blur_tile(extended, row_taps, col_taps, table_rows, table_cols):
    rows_toe = jnp.einsum('zjt,tye->zjye', row_taps.astype(jnp.float32), table_rows, precision=lax.Precision.HIGHEST)
    cols_toe = jnp.einsum('zjt,txf->zjxf', col_taps.astype(jnp.float32), table_cols, precision=lax.Precision.HIGHEST)
    passes = jnp.einsum('zjye,zef->zjyf', rows_toe, extended, precision=lax.Precision.HIGHEST)
    passes = lax.optimization_barrier(passes.astype(jnp.bfloat16)).astype(jnp.float32)
    return jnp.einsum('zjyf,zjxf->zyx', passes, cols_toe, precision=lax.Precision.HIGHEST)

def whole_pass(field_b, row_taps, col_taps, table_rows, table_cols):
    half = TAPS // 2
    padded = jnp.pad(field_b.astype(jnp.float32), ((0, 0), (half, half), (half, half)))

    def one_tile(tile_index):
        band_row = tile_index // N_COL
        band_col = tile_index % N_COL
        extended = lax.dynamic_slice(padded, (jnp.int32(0), (band_row * TR).astype(jnp.int32), (band_col * TC).astype(jnp.int32)), (DEPTH, TR + 2 * half, TC + 2 * half))
        return blur_tile(extended, row_taps[band_row, band_col], col_taps[band_row, band_col], table_rows, table_cols)
    tiles = lax.map(one_tile, jnp.arange(N_ROW * N_COL, dtype=jnp.int32))
    tiles = tiles.reshape(N_ROW, N_COL, DEPTH, TR, TC).transpose(2, 0, 3, 1, 4)
    return tiles.reshape(DEPTH, N_ROW * TR, N_COL * TC)

def reference(observed, estimate, psf_bank, zone_ids, mix_weights, illumination):
    band = psf_bank.reshape(N_ROW, ZBAND, DEPTH, 2, RANK, TAPS)
    row_pick = jnp.arange(N_ROW, dtype=jnp.int32)[:, None, None, None]
    depth_pick = jnp.arange(DEPTH, dtype=jnp.int32)[None, None, :, None]
    selected = band[row_pick, zone_ids, depth_pick]
    row_f = selected[..., 0, :, :]
    col_f = selected[..., 1, :, :]
    total = jnp.sum(mix_weights[..., None] * jnp.sum(row_f, -1) * jnp.sum(col_f, -1), axis=(-2, -1))
    row_taps = (mix_weights[..., None, None] * row_f / total[..., None, None, None]).reshape(N_ROW, N_COL, DEPTH, K * RANK, TAPS).astype(jnp.bfloat16)
    col_taps = col_f.reshape(N_ROW, N_COL, DEPTH, K * RANK, TAPS).astype(jnp.bfloat16)
    back_rows = row_taps[..., ::-1]
    back_cols = col_taps[..., ::-1]
    table_rows = band_table(TR, TAPS)
    table_cols = band_table(TC, TAPS)
    length = COARSE
    stiffness = float(length * length) / 16.0
    main_diag = jnp.full((DEPTH, length), 1.0 + 2.0 * stiffness, jnp.float32)
    main_diag = main_diag.at[:, 0].set(1.0 + stiffness).at[:, -1].set(1.0 + stiffness)
    lower_diag = jnp.full((DEPTH, length), -stiffness, jnp.float32).at[:, 0].set(0.0)
    upper_diag = jnp.full((DEPTH, length), -stiffness, jnp.float32).at[:, -1].set(0.0)
    smooth = lax.linalg.tridiagonal_solve(lower_diag, main_diag, upper_diag, illumination)
    factor = jnp.repeat(jnp.repeat(smooth, TR // CR, axis=1), TC, axis=2)
    current = estimate
    for step in range(ITERS):
        blurred = whole_pass(current.astype(jnp.bfloat16), row_taps, col_taps, table_rows, table_cols)
        ratio = (observed / blurred).astype(jnp.bfloat16)
        back = whole_pass(ratio, back_rows, back_cols, table_rows, table_cols)
        current = current * back / factor
    return current
```

```python
import functools

import jax
import jax.numpy as jnp
import numpy as np
from jax import lax
from jax.experimental import pallas as pl
from jax.experimental.pallas import tpu as pltpu
from jax.sharding import PartitionSpec as P

ITERS = 2
F32 = jnp.float32
BF16 = jnp.bfloat16
HIGHEST = lax.Precision.HIGHEST
VMEM = pl.BlockSpec(memory_space=pltpu.VMEM)
SMEM = pl.BlockSpec(memory_space=pltpu.SMEM)

TILE = 128
HALO = 16
PACK = TILE // HALO
TAP_ROWS = 48


def lanes(shape):
    return lax.broadcasted_iota(jnp.int32, shape, len(shape) - 1)


def sublanes(shape):
    return lax.broadcasted_iota(jnp.int32, shape, len(shape) - 2)


def call(body, outs, specs, scratch=(), name=None, flops=0):
    return pl.pallas_call(
        body,
        out_shape=outs,
        in_specs=specs,
        out_specs=jax.tree.map(lambda _: VMEM, outs),
        scratch_shapes=list(scratch),
        compiler_params=pltpu.CompilerParams(vmem_limit_bytes=16 * 1024 * 1024),
        cost_estimate=pl.CostEstimate(flops=flops, bytes_accessed=1 << 20, transcendentals=0),
        name=name,
    )


def shift(cells, axis, by):
    count = lax.axis_size(axis)
    return lax.ppermute(cells, axis, [(i, (i + by) % count) for i in range(count)])


def gathered(piece, axis):
    count = lax.axis_size(axis)
    if count <= 8:
        return [piece] + [shift(piece, axis, s) for s in range(1, count)]
    every = lax.all_gather(piece, axis, axis=0)
    me = lax.axis_index(axis)
    return [lax.dynamic_index_in_dim(every, (me - s) % count, 0, False) for s in range(count)]


def bank_kernel(bank_ref, out_ref):
    rows, taps = bank_ref.shape
    for block in range(rows // TILE):
        part = bank_ref[block * TILE : (block + 1) * TILE, :]
        part = jnp.concatenate([part, jnp.zeros((TILE, TILE - taps), F32)], axis=1)
        out_ref[:, block * TILE : (block + 1) * TILE] = part.T[:TAP_ROWS].astype(BF16)


def taps_kernel(cols, taps, meta_ref, ids_ref, mix_ref, *refs):
    pieces, uv_ref = refs[:cols], refs[cols]
    col = meta_ref[5]
    blended = ids_ref.shape[0]
    zones = pieces[0].shape[1] // TILE
    lane = lanes((1, TILE))
    is_row = (lane & 7) < 4
    picked = []
    total = jnp.zeros((1, TILE), F32)
    for k in range(blended):
        ids = ids_ref[k : k + 1, :]
        got = jnp.zeros((TAP_ROWS, TILE), F32)
        for s in range(cols):
            first = lax.rem(col + cols - s, cols) * zones
            for m in range(zones):
                got = jnp.where(
                    ids == first + m,
                    pieces[s][:, m * TILE : (m + 1) * TILE].astype(F32),
                    got,
                )
        sums = jnp.sum(got, axis=0, keepdims=True)
        both = sums * pltpu.roll(sums, TILE - 4, 1)
        total = total + jnp.where(is_row, both * mix_ref[k : k + 1, :], 0.0)
        picked.append(got)
    group = (lanes((TILE, TILE)) >> 3) == (sublanes((TILE, TILE)) >> 3)
    total = jnp.dot(
        jnp.broadcast_to(total, (8, TILE)),
        group.astype(F32),
        precision=HIGHEST,
        preferred_element_type=F32,
    )[:1]
    tap = sublanes((TAP_ROWS, 2 * TILE))
    at = lanes((TAP_ROWS, 2 * TILE))
    half = taps // 2
    goes = jnp.where(at < TILE, (tap - half) & (TILE - 1), TILE + ((half - tap) & (TILE - 1)))
    place = ((goes == at) & (tap < taps)).astype(F32).astype(BF16)
    for k in range(blended):
        got = picked[k]
        scaled = mix_ref[k : k + 1, :] * got / total
        chosen = jnp.where(is_row, scaled, got).astype(BF16)
        uv_ref[k] = lax.dot_general(
            chosen, place, (((0,), (0,)), ((), ())), preferred_element_type=F32
        ).reshape(uv_ref.shape[1:])


def turned(uv_ref, z, k, r, part, rows, by):
    line = uv_ref[k, z, r : r + 1, part * TILE : (part + 1) * TILE]
    return pltpu.roll(
        jnp.broadcast_to(line, (rows, TILE)), by % TILE, 1, stride=1, stride_axis=0
    )


def bands_kernel(part, rows, meta_ref, uv_ref, *refs):
    if part == 0:
        ct_ref, rt_ref, edge_ref = refs
    else:
        inverse_ref, illum, (ct_ref, rt_ref, edge_ref, inv_ref) = refs[0], refs[1 : 1 + rows], refs[1 + rows :]
        coarse = illum[0].shape[0]
        smooth = jnp.zeros((TILE, illum[0].shape[1]), F32)
        for s in range(rows):
            first = pl.multiple_of(lax.rem(meta_ref[4] + rows - s, rows) * coarse, coarse)
            smooth = smooth + lax.dot_general(
                inverse_ref[meta_ref[4], pl.ds(first, coarse), :],
                illum[s][...],
                (((0,), (0,)), ((), ())),
                precision=HIGHEST,
                preferred_element_type=F32,
            )
        inv = 1.0 / smooth
        for g in range(inv_ref.shape[0]):
            inv_ref[g] = inv[:, g * PACK : (g + 1) * PACK]
    lane = lanes((HALO, TILE))
    low = lane < TILE // 2
    none = jnp.zeros((HALO, TILE), F32)
    zero = jnp.zeros((HALO, 8 * TILE), BF16)

    def one(z, carry):
        at = lax.rem(z, PACK)
        for t in range(PACK):
            ct_ref[z, TILE + t * HALO : TILE + (t + 1) * HALO, :] = zero
        left = pl.multiple_of(TILE + at * HALO, HALO)
        right = pl.multiple_of(TILE + ((at + 4) & 7) * HALO, HALO)
        for j in range(8):
            here = slice(j * TILE, (j + 1) * TILE)
            full = turned(uv_ref, z, j // 4, 4 + j % 4, 1 - part, TILE, 0)
            first, last = full[:HALO], full[TILE - HALO :]
            ct_ref[z, :HALO, here] = jnp.where(low, first, none).astype(BF16)
            ct_ref[z, HALO : TILE - HALO, here] = full[HALO : TILE - HALO].astype(BF16)
            ct_ref[z, TILE - HALO : TILE, here] = jnp.where(low, none, last).astype(BF16)
            ct_ref[z, pl.ds(left, HALO), here] = jnp.where(low, last, none).astype(BF16)
            ct_ref[z, pl.ds(right, HALO), here] = jnp.where(low, none, first).astype(BF16)
        above, below = [none, none], [none, none]
        for j in range(8):
            here = slice(j * TILE, (j + 1) * TILE)
            full = turned(uv_ref, z, j // 4, j % 4, part, TILE, 0)
            first, last = full[:HALO], full[TILE - HALO :]
            rt_ref[z, :HALO, here] = jnp.where(low, first, none).astype(BF16)
            rt_ref[z, HALO : TILE - HALO, here] = full[HALO : TILE - HALO].astype(BF16)
            rt_ref[z, TILE - HALO :, here] = jnp.where(low, none, last).astype(BF16)
            spot = (j % 4) * 2
            up = turned(uv_ref, z, j // 4, j % 4, part, HALO, (spot + 1) * HALO)
            down = turned(uv_ref, z, j // 4, j % 4, part, HALO, spot * HALO)
            above[j // 4] = jnp.where(lane >> 4 == spot, up, above[j // 4])
            below[j // 4] = jnp.where(lane >> 4 == spot + 1, down, below[j // 4])
        edge_ref[z] = jnp.concatenate(
            [jnp.concatenate(above, axis=1), jnp.concatenate(below, axis=1)], axis=0
        ).astype(BF16)
        return carry

    lax.fori_loop(0, ct_ref.shape[0], one, 0)


def joined_halo(left, right, parity, meta_ref):
    lane = lanes(left.shape)
    take_left = (lane < TILE // 2) == (parity == 0)
    left = jnp.where(meta_ref[0] > 0, left, jnp.zeros_like(left))
    right = jnp.where(meta_ref[1] > 0, right, jnp.zeros_like(right))
    return jnp.where(take_left, left, right)


def pack_strips(value, i, g8, rows, lr_ref, rr_ref):
    lane = lanes(value.shape) >> 4
    at = (i + 4) % PACK
    to_right = pltpu.roll(value, (i * HALO - 112) % TILE, 1)
    to_left = pltpu.roll(value, at * HALO, 1)
    if i == 0:
        rr_ref[g8, rows] = to_right
        lr_ref[g8, rows] = to_left
    else:
        rr_ref[g8, rows] = jnp.where(lane == i, to_right, rr_ref[g8, rows])
        lr_ref[g8, rows] = jnp.where(lane == at, to_left, lr_ref[g8, rows])


def finish(part, blurred, g8, i, rows, a_ref, inv_ref, outs):
    z = g8 * PACK + i
    if part == 0:
        value = a_ref[z, rows] / blurred
    else:
        value = a_ref[z, rows] * blurred * inv_ref[g8, rows, i : i + 1]
        outs[0][z, rows] = value
        outs = outs[1:]
    if outs:
        b_ref, lr_ref, rr_ref = outs
        value = value.astype(BF16)
        b_ref[z, rows] = value
        pack_strips(value, i, g8, rows, lr_ref, rr_ref)


def main_kernel(part, meta_ref, ct_ref, rt_ref, field_ref, left_ref, right_ref, a_ref, inv_ref, rim_ref, *refs):
    outs, q_ref = refs[:-1], refs[-1]
    inner = slice(HALO, TILE - HALO)

    def group(g8, carry):
        halos = [joined_halo(left_ref[g8], right_ref[g8], parity, meta_ref) for parity in range(2)]

        def columns(i):
            wide = jnp.concatenate([field_ref[g8 * PACK + i], halos[i // 4]], axis=1)
            for n in range(4):
                got = jnp.dot(
                    wide, ct_ref[g8 * PACK + i, :, n * 256 : (n + 1) * 256], preferred_element_type=F32
                ).astype(BF16)
                q_ref[i % 4, n * 256 : n * 256 + TILE, :] = got[:, :TILE]
                q_ref[i % 4, n * 256 + TILE : (n + 1) * 256, :] = got[:, TILE:]

        def rows(i):
            z = g8 * PACK + i
            blurred = jnp.dot(rt_ref[z], q_ref[i % 4], preferred_element_type=F32)
            rim_ref[z, :HALO] = blurred[:HALO]
            rim_ref[z, HALO:] = blurred[TILE - HALO :]
            finish(part, blurred[inner], g8, i, inner, a_ref, inv_ref, outs)

        columns(0)
        for i in range(PACK):
            if i + 1 < PACK:
                columns(i + 1)
            rows(i)
        return carry

    lax.fori_loop(0, field_ref.shape[0] // PACK, group, 0)


def edge_kernel(part, meta_ref, ct_ref, edge_ref, rim_ref, top_ref, bot_ref, a_ref, inv_ref, *refs):
    count = len(refs) // 2
    made, outs, q_ref = refs[:count], refs[count:-1], refs[-1]
    depth = rim_ref.shape[0]
    inner = slice(HALO, TILE - HALO)

    def group(g8, carry):
        halos = [
            [joined_halo(ref[depth + g8], ref[depth + 2 + g8], parity, meta_ref) for parity in range(2)]
            for ref in (top_ref, bot_ref)
        ]
        for old, new in zip(made, outs):
            each = pl.ds(g8 * (new.shape[0] // (depth // PACK)), new.shape[0] // (depth // PACK))
            new[each, inner] = old[each, inner]

        def columns(i):
            z = g8 * PACK + i
            sides = []
            for s, ref in enumerate((top_ref, bot_ref)):
                side = jnp.concatenate([ref[z], halos[s][i // 4]], axis=1)
                sides.append(jnp.where(meta_ref[2 + s] > 0, side, jnp.zeros_like(side)))
            wide = jnp.concatenate(sides, axis=0)
            for n in range(4):
                got = jnp.dot(
                    wide, ct_ref[z, :, n * 256 : (n + 1) * 256], preferred_element_type=F32
                ).astype(BF16)
                q_ref[i % 4, n * 64 : n * 64 + 32, :] = got[:, :TILE]
                q_ref[i % 4, n * 64 + 32 : (n + 1) * 64, :] = got[:, TILE:]

        def rows(i):
            z = g8 * PACK + i
            blurred = rim_ref[z] + jnp.dot(edge_ref[z], q_ref[i % 4], preferred_element_type=F32)
            for s, at in enumerate((slice(0, HALO), slice(TILE - HALO, TILE))):
                finish(part, blurred[s * HALO : (s + 1) * HALO], g8, i, at, a_ref, inv_ref, outs)

        columns(0)
        for i in range(PACK):
            if i + 1 < PACK:
                columns(i + 1)
            rows(i)
        return carry

    lax.fori_loop(0, depth // PACK, group, 0)


def first_kernel(est_ref, b_ref, lr_ref, rr_ref):
    def group(g8, carry):
        for i in range(PACK):
            value = est_ref[g8 * PACK + i].astype(BF16)
            b_ref[g8 * PACK + i] = value
            pack_strips(value, i, g8, slice(0, TILE), lr_ref, rr_ref)
        return carry

    lax.fori_loop(0, est_ref.shape[0] // PACK, group, 0)


def smoothing(length, rows):
    stiffness = float(length * length) / 16.0
    d = np.diff(np.eye(length), axis=0)
    inverse = np.linalg.inv(np.eye(length) + stiffness * d.T @ d)
    wide = np.repeat(inverse, TILE * rows // length, axis=0)
    return jnp.asarray(wide.reshape(rows, TILE, length).transpose(0, 2, 1), F32)


def shards(observed, estimate, psf_bank, zone_ids, mix_weights, illumination):
    depth = estimate.shape[0]
    zones_here, _, _, rank, taps = psf_bank.shape
    n_row, n_col = lax.axis_size("row"), lax.axis_size("col")
    row, col = lax.axis_index("row"), lax.axis_index("col")
    groups = depth // PACK
    flag = lambda x: x.astype(jnp.int32)
    meta = jnp.stack(
        [flag(col > 0), flag(col < n_col - 1), flag(row > 0), flag(row < n_row - 1), flag(row), flag(col)]
    )
    volume = jax.ShapeDtypeStruct((depth, TILE, TILE), F32)
    narrow = jax.ShapeDtypeStruct((depth, TILE, TILE), BF16)
    strip = jax.ShapeDtypeStruct((groups, TILE, TILE), BF16)

    bank = call(
        bank_kernel, jax.ShapeDtypeStruct((TAP_ROWS, zones_here * TILE), BF16), [VMEM], name="bank"
    )(psf_bank.reshape(zones_here * depth * 2 * rank, taps))
    pieces = gathered(bank, "col")
    profiles = gathered(illumination[:, :, 0].T, "row")
    per_lane = lambda x: jnp.repeat(x[0, 0].T, 2 * rank, axis=1)
    inverse = smoothing(illumination.shape[1] * n_row, n_row)
    uv = call(
        functools.partial(taps_kernel, n_col, taps),
        jax.ShapeDtypeStruct((zone_ids.shape[-1], depth, 2 * rank, 2 * TILE), F32),
        [SMEM] + [VMEM] * (2 + n_col),
        name="taps",
    )(meta, per_lane(zone_ids), per_lane(mix_weights), *pieces)

    def bands(part, uv):
        shape = lambda *s: jax.ShapeDtypeStruct((depth,) + s, BF16)
        outs = (shape(2 * TILE, 8 * TILE), shape(TILE, 8 * TILE), shape(2 * HALO, 2 * TILE))
        args = [meta, uv]
        if part == 1:
            outs = outs + (jax.ShapeDtypeStruct((groups, TILE, PACK), F32),)
            args = args + [inverse] + profiles
        return call(
            functools.partial(bands_kernel, part, n_row),
            outs,
            [SMEM] + [VMEM] * (len(args) - 1),
            name="bands",
            flops=4 * 10**9,
        )(*args)

    def blur(part, last, made, field, lr, rr, other):
        ct, rt, edge, inv = made
        left, right = shift(rr, "col", 1), shift(lr, "col", -1)
        ends = [
            jnp.concatenate([field[:, rows], left[:, rows], right[:, rows]], axis=0)
            for rows in (slice(0, HALO), slice(TILE - HALO, TILE))
        ]
        bot, top = shift(ends[0], "row", -1), shift(ends[1], "row", 1)
        rim = jax.ShapeDtypeStruct((depth, 2 * HALO, TILE), F32)
        outs = ((volume,) if part == 1 else ()) + (() if last else (narrow, strip, strip))
        main, *got = call(
            functools.partial(main_kernel, part),
            (rim,) + outs,
            [SMEM] + [VMEM] * 7,
            [pltpu.VMEM((4, 8 * TILE, TILE), BF16)],
            name="main",
            flops=4 * 10**9,
        )(meta, ct, rt, field, left, right, other, inv)
        return call(
            functools.partial(edge_kernel, part),
            outs,
            [SMEM] + [VMEM] * (7 + len(outs)),
            [pltpu.VMEM((4, 2 * TILE, TILE), BF16)],
            name="edge",
            flops=2 * 10**9,
        )(meta, ct, edge, main, top, bot, other, inv, *got)

    current = estimate
    field, lr, rr = call(first_kernel, (narrow, strip, strip), [VMEM], name="first")(estimate)
    unused = jnp.zeros((groups, TILE, PACK), F32)
    forward = (*bands(0, uv), unused)
    backward = None
    for step in range(ITERS):
        last = step == ITERS - 1
        ratio, lr, rr = blur(0, False, forward, field, lr, rr, observed)
        if backward is None:
            backward = bands(1, lax.optimization_barrier((uv, lr))[0])
        current, *rest = blur(1, last, backward, ratio, lr, rr, current)
        if not last:
            field, lr, rr = rest
    return current


def solution(mesh):
    placed = (
        P(None, "row", "col"),
        P(None, "row", "col"),
        P(("row", "col"), None, None, None, None),
        P("row", "col", None, None),
        P("row", "col", None, None),
        P(None, "row", "col"),
    )
    return jax.shard_map(
        shards, mesh=mesh, in_specs=placed, out_specs=P(None, "row", "col"), check_vma=False
    )
```

```python
import functools

import jax
import jax.numpy as jnp
import numpy as np
from jax import lax
from jax.experimental import pallas as pl
from jax.experimental.pallas import tpu as pltpu
from jax.sharding import PartitionSpec as P

ITERS = 2
F32 = jnp.float32
BF16 = jnp.bfloat16
HIGHEST = lax.Precision.HIGHEST
VMEM = pl.BlockSpec(memory_space=pltpu.VMEM)
SMEM = pl.BlockSpec(memory_space=pltpu.SMEM)

TILE = 128
HALO = 16
PACK = TILE // HALO
TAP_ROWS = 48


def lanes(shape):
    return lax.broadcasted_iota(jnp.int32, shape, len(shape) - 1)


def sublanes(shape):
    return lax.broadcasted_iota(jnp.int32, shape, len(shape) - 2)


def call(body, outs, specs, scratch=(), name=None, flops=0, mib=16):
    return pl.pallas_call(
        body,
        out_shape=outs,
        in_specs=specs,
        out_specs=jax.tree.map(lambda _: VMEM, outs),
        scratch_shapes=list(scratch),
        compiler_params=pltpu.CompilerParams(vmem_limit_bytes=mib * 1024 * 1024),
        cost_estimate=pl.CostEstimate(flops=flops, bytes_accessed=1 << 20, transcendentals=0),
        name=name,
    )


def shift(cells, axis, by):
    count = lax.axis_size(axis)
    return lax.ppermute(cells, axis, [(i, (i + by) % count) for i in range(count)])


def swap(cells, axis, pairs):
    return lax.ppermute(cells, axis, pairs + [(j, i) for i, j in pairs])


def gathered(piece, axis):
    count = lax.axis_size(axis)
    if count <= 8:
        return [piece] + [shift(piece, axis, s) for s in range(1, count)]
    every = lax.all_gather(piece, axis, axis=0)
    me = lax.axis_index(axis)
    return [lax.dynamic_index_in_dim(every, (me - s) % count, 0, False) for s in range(count)]


def swap_pairs(cells, axis):
    return swap(cells, axis, [(i, i + 1) for i in range(0, lax.axis_size(axis), 2)])


def bank_kernel(bank_ref, ids_ref, mix_ref, out_ref, keys_ref):
    rows, taps = bank_ref.shape
    for block in range(rows // TILE):
        part = bank_ref[block * TILE : (block + 1) * TILE, :]
        part = jnp.concatenate([part, jnp.zeros((TILE, TILE - taps), F32)], axis=1)
        out_ref[:, block * TILE : (block + 1) * TILE] = part.T[:TAP_ROWS].astype(BF16)
    spread = (lanes((ids_ref.shape[1], TILE)) >> 3 == sublanes((ids_ref.shape[1], TILE))).astype(F32)
    both = jnp.concatenate([ids_ref[...].astype(F32), mix_ref[...]], axis=0)
    keys_ref[...] = jnp.dot(both, spread, precision=HIGHEST, preferred_element_type=F32)


def pick_kernel(cols, meta_ref, mine_ref, other_ref, *refs):
    pieces, outs = refs[:-2], refs[-2:]
    zones = pieces[0].shape[1] // TILE
    for keys_ref, out_ref in zip((mine_ref, other_ref), outs):
        ids = (keys_ref[...] + 0.5).astype(jnp.int32)
        for k in range(out_ref.shape[0]):
            got = jnp.zeros((TAP_ROWS, TILE), F32)
            for s, piece in enumerate(pieces):
                first = lax.rem(meta_ref[5] + cols - 2 * s, cols) * zones
                for m in range(zones):
                    got = jnp.where(
                        ids[k : k + 1] == first + m, piece[:, m * TILE : (m + 1) * TILE].astype(F32), got
                    )
            out_ref[k] = got.astype(BF16)


def taps_kernel(taps, keys_ref, mine_ref, other_ref, uv_ref):
    blended = mine_ref.shape[0]
    lane = lanes((1, TILE))
    is_row = (lane & 7) < 4
    picked = []
    total = jnp.zeros((1, TILE), F32)
    mix = keys_ref[blended:, :]
    for k in range(blended):
        got = mine_ref[k].astype(F32) + other_ref[k].astype(F32)
        sums = jnp.sum(got, axis=0, keepdims=True)
        both = sums * pltpu.roll(sums, TILE - 4, 1)
        total = total + jnp.where(is_row, both * mix[k : k + 1], 0.0)
        picked.append(got)
    group = (lanes((TILE, TILE)) >> 3) == (sublanes((TILE, TILE)) >> 3)
    total = jnp.dot(
        jnp.broadcast_to(total, (8, TILE)),
        group.astype(F32),
        precision=HIGHEST,
        preferred_element_type=F32,
    )[:1]
    tap = sublanes((TAP_ROWS, 2 * TILE))
    at = lanes((TAP_ROWS, 2 * TILE))
    half = taps // 2
    goes = jnp.where(at < TILE, (tap - half) & (TILE - 1), TILE + ((half - tap) & (TILE - 1)))
    place = ((goes == at) & (tap < taps)).astype(F32).astype(BF16)
    for k in range(blended):
        got = picked[k]
        scaled = mix[k : k + 1] * got / total
        chosen = jnp.where(is_row, scaled, got).astype(BF16)
        uv_ref[k] = lax.dot_general(
            chosen, place, (((0,), (0,)), ((), ())), preferred_element_type=F32
        ).reshape(uv_ref.shape[1:])


def turned(uv_ref, z, k, r, part, rows, by):
    line = uv_ref[k, z, r : r + 1, part * TILE : (part + 1) * TILE]
    return pltpu.roll(
        jnp.broadcast_to(line, (rows, TILE)), by % TILE, 1, stride=1, stride_axis=0
    )


def bands_kernel(part, rows, meta_ref, uv_ref, *refs):
    *refs, shifts_ref = refs
    if part == 0:
        (ct_ref,) = refs
    else:
        inverse_ref, illum, (ct_ref, inv_ref) = refs[0], refs[1 : 1 + rows], refs[1 + rows :]
        coarse = illum[0].shape[2]
        smooth = jnp.zeros((TILE, illum[0].shape[0]), F32)
        for s in range(rows):
            first = pl.multiple_of(lax.rem(meta_ref[4] + rows - s, rows) * coarse, coarse)
            smooth = smooth + lax.dot_general(
                inverse_ref[meta_ref[4], pl.ds(first, coarse), :],
                illum[s][:, 0, :].T,
                (((0,), (0,)), ((), ())),
                precision=HIGHEST,
                preferred_element_type=F32,
            )
        inv = 1.0 / smooth
        for g in range(inv_ref.shape[0]):
            inv_ref[g] = inv[:, g * PACK : (g + 1) * PACK]
    low_all = lanes((TILE, TILE)) < TILE // 2
    none = jnp.zeros((TILE, TILE), BF16)
    for t in range(PACK):
        to = (sublanes((TILE, TILE)) + t * HALO) & (TILE - 1)
        shifts_ref[:, t * TILE : (t + 1) * TILE] = (to == lanes((TILE, TILE))).astype(F32).astype(BF16)
    ct_ref[:, TILE:, :] = jnp.zeros((ct_ref.shape[0], TILE, 8 * TILE), BF16)

    def group(g8, carry):
        for i in range(PACK):
            z = g8 * PACK + i
            left, right = TILE + i * HALO, TILE + (i + 4) % PACK * HALO
            base = [turned(uv_ref, z, j // 4, 4 + j % 4, 1 - part, HALO, 0) for j in range(8)]
            base = jnp.concatenate(base, axis=0).astype(BF16)
            for t in range(0, PACK, 2):
                got = jnp.dot(
                    base, shifts_ref[:, t * TILE : (t + 2) * TILE], preferred_element_type=F32
                ).astype(BF16)
                first, second = got[:, :TILE], got[:, TILE:]
                if t == 0:
                    first, after = jnp.where(low_all, first, none), jnp.where(low_all, none, first)
                elif t == PACK - 2:
                    second, before = jnp.where(low_all, none, second), jnp.where(low_all, second, none)
                for j in range(8):
                    here, rows = slice(j * TILE, (j + 1) * TILE), slice(j * HALO, (j + 1) * HALO)
                    ct_ref[z, t * HALO : (t + 1) * HALO, here] = first[rows]
                    ct_ref[z, (t + 1) * HALO : (t + 2) * HALO, here] = second[rows]
                    if t == 0:
                        ct_ref[z, right : right + HALO, here] = after[rows]
                    elif t == PACK - 2:
                        ct_ref[z, left : left + HALO, here] = before[rows]
        return carry

    lax.fori_loop(0, ct_ref.shape[0] // PACK, group, 0)


def other_bands(part, uv_ref, ct_ref, z, i, cw_ref, rt_ref, edge_ref):
    low = lanes((HALO, TILE)) < TILE // 2
    lane = lanes((HALO, TILE)) >> 4
    none = jnp.zeros((HALO, TILE), F32)
    above, below = [none] * 2, [none] * 2
    for j in range(8):
        here = slice(j * TILE, (j + 1) * TILE)
        full = turned(uv_ref, z, j // 4, j % 4, part, TILE, 0)
        first, last = full[:HALO], full[TILE - HALO :]
        rt_ref[z, :HALO, here] = jnp.where(low, first, none).astype(BF16)
        rt_ref[z, HALO : TILE - HALO, here] = full[HALO : TILE - HALO].astype(BF16)
        rt_ref[z, TILE - HALO :, here] = jnp.where(low, none, last).astype(BF16)
        spot = (j % 4) * 2
        above[j // 4] = jnp.where(lane == spot, full[(spot + 1) * HALO : (spot + 2) * HALO], above[j // 4])
        below[j // 4] = jnp.where(lane == spot + 1, full[spot * HALO : (spot + 1) * HALO], below[j // 4])
    edge_ref[z] = jnp.concatenate(
        [jnp.concatenate(above, axis=1), jnp.concatenate(below, axis=1)], axis=0
    ).astype(BF16)
    before, after = TILE + i * HALO, TILE + (i + 4) % PACK * HALO
    cw_ref[z, TILE - 2 * HALO :, :] = jnp.zeros((2 * HALO, 4 * TILE), BF16)
    for j in range(0, 8, 2):
        this, other = slice(j * TILE, (j + 1) * TILE), slice((j + 1) * TILE, (j + 2) * TILE)
        for t in range(6):
            a = before if t == 0 else (t - 1) * HALO
            b = after if t == 5 else (t + 3) * HALO
            cw_ref[z, t * HALO : (t + 1) * HALO, j * TILE // 2 : j * TILE // 2 + TILE] = jnp.where(
                low, ct_ref[z, a : a + HALO, this], ct_ref[z, b : b + HALO, other]
            )


def sides_of(left, right, meta_ref):
    left = jnp.where(meta_ref[0] > 0, left, jnp.zeros_like(left))
    right = jnp.where(meta_ref[1] > 0, right, jnp.zeros_like(right))
    return left, right


def joined(left, right, parity):
    low = lanes(left.shape) < TILE // 2
    return jnp.where(low, left, right) if parity == 0 else jnp.where(low, right, left)


def windows(field, left, right, i):
    lane = lanes(field.shape)
    left = pltpu.roll(left, -i * HALO % TILE, 1)
    right = pltpu.roll(right, (80 - (i + 4) % PACK * HALO) % TILE, 1)
    first = jnp.where(lane < HALO, left, pltpu.roll(field, HALO, 1))
    second = jnp.where(lane < 80, pltpu.roll(field, 80, 1), right)
    return first, second


def column_pass(wide, cw_ref, z, q_ref, slot):
    rows = wide.shape[0] // 2
    low = lanes((rows, TILE)) < TILE // 2
    for n in range(2):
        got = jnp.dot(
            wide, cw_ref[z, :, n * 256 : (n + 1) * 256], preferred_element_type=F32
        ).astype(BF16)
        for p in range(2):
            first, second = got[:rows, p * TILE : (p + 1) * TILE], got[rows:, p * TILE : (p + 1) * TILE]
            at = (n * 4 + p * 2) * rows
            q_ref[slot, at : at + rows, :] = jnp.where(low, first, pltpu.roll(second, TILE // 2, 1))
            q_ref[slot, at + rows : at + 2 * rows, :] = jnp.where(low, pltpu.roll(first, TILE // 2, 1), second)


def pack_strips(value, i, g8, rows, right_ref, left_ref):
    lane = lanes(value.shape) >> 4
    at = (i + 4) % PACK
    to_right = pltpu.roll(value, (i * HALO - 112) % TILE, 1)
    to_left = pltpu.roll(value, at * HALO, 1)
    if i == 0:
        right_ref[g8, rows] = to_right
        left_ref[g8, rows] = to_left
    else:
        right_ref[g8, rows] = jnp.where(lane == i, to_right, right_ref[g8, rows])
        left_ref[g8, rows] = jnp.where(lane == at, to_left, left_ref[g8, rows])


def finish(part, blurred, g8, i, rows, a_ref, inv_ref, outs):
    z = g8 * PACK + i
    if part == 0:
        value = a_ref[z, rows] / blurred
    else:
        value = a_ref[z, rows] * blurred * inv_ref[g8, rows, i : i + 1]
        outs[0][z, rows] = value
        outs = outs[1:]
    if outs:
        b_ref, right_ref, left_ref = outs
        value = value.astype(BF16)
        b_ref[z, rows] = value
        pack_strips(value, i, g8, rows, right_ref, left_ref)


def main_kernel(part, making, meta_ref, ct_ref, rt_ref, field_ref, left_ref, right_ref, a_ref, inv_ref, rim_ref, *refs):
    outs, q_ref = refs[:-1], refs[-1]
    if making:
        outs, made, uv_ref, rt_ref = outs[:-3], outs[-3:], rt_ref, outs[-2]
    inner = slice(HALO, TILE - HALO)

    def group(g8, carry):
        sides = sides_of(left_ref[g8], right_ref[g8], meta_ref)
        halos = [joined(*sides, parity) for parity in range(2)]

        def columns(i):
            if making:
                other_bands(part, uv_ref, ct_ref, g8 * PACK + i, i, *made)
            wide = jnp.concatenate([field_ref[g8 * PACK + i], halos[i // 4]], axis=1)
            for n in range(4):
                got = jnp.dot(
                    wide, ct_ref[g8 * PACK + i, :, n * 256 : (n + 1) * 256], preferred_element_type=F32
                ).astype(BF16)
                q_ref[i % 4, n * 256 : n * 256 + TILE, :] = got[:, :TILE]
                q_ref[i % 4, n * 256 + TILE : (n + 1) * 256, :] = got[:, TILE:]

        def rows(i):
            z = g8 * PACK + i
            blurred = jnp.dot(rt_ref[z], q_ref[i % 4], preferred_element_type=F32)
            rim_ref[z, :HALO] = blurred[:HALO]
            rim_ref[z, HALO:] = blurred[TILE - HALO :]
            finish(part, blurred[inner], g8, i, inner, a_ref, inv_ref, outs)

        columns(0)
        columns(1)
        for i in range(PACK):
            if i + 2 < PACK:
                columns(i + 2)
            rows(i)
        return carry

    for g8 in range(field_ref.shape[0] // PACK):
        group(g8, 0)


def edge_kernel(part, meta_ref, cw_ref, edge_ref, rim_ref, top_ref, bot_ref, a_ref, inv_ref, *refs):
    count = len(refs) // 2
    made, outs, q_ref = refs[:count], refs[count:-1], refs[-1]
    depth = rim_ref.shape[0]
    inner = slice(HALO, TILE - HALO)

    def group(g8, carry):
        halos = [sides_of(ref[depth + g8], ref[depth + 2 + g8], meta_ref) for ref in (top_ref, bot_ref)]
        for old, new in zip(made, outs):
            each = pl.ds(g8 * (new.shape[0] // (depth // PACK)), new.shape[0] // (depth // PACK))
            new[each, inner] = old[each, inner]

        def columns(i):
            z = g8 * PACK + i
            pairs = []
            for s, ref in enumerate((top_ref, bot_ref)):
                both = windows(ref[z], *halos[s], i)
                pairs.append([jnp.where(meta_ref[2 + s] > 0, w, jnp.zeros_like(w)) for w in both])
            wide = jnp.concatenate([pairs[0][0], pairs[1][0], pairs[0][1], pairs[1][1]], axis=0)
            column_pass(wide, cw_ref, z, q_ref, i)

        def rows(i):
            z = g8 * PACK + i
            blurred = rim_ref[z] + jnp.dot(edge_ref[z], q_ref[i], preferred_element_type=F32)
            for s, at in enumerate((slice(0, HALO), slice(TILE - HALO, TILE))):
                finish(part, blurred[s * HALO : (s + 1) * HALO], g8, i, at, a_ref, inv_ref, outs)

        for i in range(PACK):
            columns(i)
        for i in range(PACK):
            rows(i)
        return carry

    for g8 in range(depth // PACK):
        group(g8, 0)


def first_kernel(est_ref, b_ref, right_ref, left_ref):
    def group(g8, carry):
        for i in range(PACK):
            value = est_ref[g8 * PACK + i].astype(BF16)
            b_ref[g8 * PACK + i] = value
            pack_strips(value, i, g8, slice(0, TILE), right_ref, left_ref)
        return carry

    lax.fori_loop(0, est_ref.shape[0] // PACK, group, 0)


def smoothing(length, rows):
    stiffness = float(length * length) / 16.0
    d = np.diff(np.eye(length), axis=0)
    inverse = np.linalg.inv(np.eye(length) + stiffness * d.T @ d)
    wide = np.repeat(inverse, TILE * rows // length, axis=0)
    return jnp.asarray(wide.reshape(rows, TILE, length).transpose(0, 2, 1), F32)


def shards(observed, estimate, psf_bank, zone_ids, mix_weights, illumination):
    depth = estimate.shape[0]
    zones_here, _, _, rank, taps = psf_bank.shape
    n_row, n_col = lax.axis_size("row"), lax.axis_size("col")
    row, col = lax.axis_index("row"), lax.axis_index("col")
    groups = depth // PACK
    flag = lambda x: x.astype(jnp.int32)
    meta = jnp.stack(
        [flag(col > 0), flag(col < n_col - 1), flag(row > 0), flag(row < n_row - 1), flag(row), flag(col)]
    )
    volume = jax.ShapeDtypeStruct((depth, TILE, TILE), F32)
    narrow = jax.ShapeDtypeStruct((depth, TILE, TILE), BF16)
    strip = jax.ShapeDtypeStruct((groups, TILE, TILE), BF16)


    def exchanged(to_right, to_left):
        return shift(to_right, "col", 1), shift(to_left, "col", -1)

    blended = zone_ids.shape[-1]
    flat = (zones_here * depth * 2 * rank, taps)
    bank, keys = call(
        bank_kernel,
        (
            jax.ShapeDtypeStruct((TAP_ROWS, zones_here * TILE), BF16),
            jax.ShapeDtypeStruct((2 * blended, TILE), F32),
        ),
        [VMEM] * 3,
        name="bank",
    )(psf_bank.reshape(flat), zone_ids[0, 0].T, mix_weights[0, 0].T)
    pieces = [bank] + [shift(bank, "col", s) for s in range(2, n_col, 2)]
    other_keys = swap_pairs(keys, "col")
    field, to_right, to_left = call(
        first_kernel, (narrow, strip, strip), [VMEM], name="first"
    )(estimate)
    left, right = exchanged(to_right, to_left)
    inverse = smoothing(illumination.shape[1] * n_row, n_row)
    factors = jax.ShapeDtypeStruct((blended, TAP_ROWS, TILE), BF16)
    mine, others = call(
        functools.partial(pick_kernel, n_col),
        (factors, factors),
        [SMEM] + [VMEM] * (2 + len(pieces)),
        name="pick",
    )(meta, keys, other_keys, *pieces)
    uv = call(
        functools.partial(taps_kernel, taps),
        jax.ShapeDtypeStruct((blended, depth, 2 * rank, 2 * TILE), F32),
        [VMEM] * 3,
        name="taps",
    )(keys, mine, swap_pairs(others, "col"))

    shape = lambda *s: jax.ShapeDtypeStruct((depth,) + s, BF16)

    def bands(part, uv):
        outs = (shape(2 * TILE, 8 * TILE),)
        args = [meta, uv]
        if part == 1:
            outs = outs + (jax.ShapeDtypeStruct((groups, TILE, PACK), F32),)
            args = args + [inverse] + profiles
        return call(
            functools.partial(bands_kernel, part, n_row),
            outs,
            [SMEM] + [VMEM] * (len(args) - 1),
            [pltpu.VMEM((TILE, 8 * TILE), BF16)],
            name="bands",
            flops=4 * 10**9,
        )(*args)

    def ends_of(field, left, right):
        return [
            jnp.concatenate([field[:, rows], left[:, rows], right[:, rows]], axis=0)
            for rows in (slice(0, HALO), slice(TILE - HALO, TILE))
        ]

    def blur(part, last, made, field, left, right, ends, other):
        ct, inv, *ready = made
        making = () if ready else (shape(TILE, 4 * TILE), shape(TILE, 8 * TILE), shape(2 * HALO, 2 * TILE))
        bot, top = shift(ends[0], "row", -1), shift(ends[1], "row", 1)
        rim = jax.ShapeDtypeStruct((depth, 2 * HALO, TILE), F32)
        outs = ((volume,) if part == 1 else ()) + (() if last else (narrow, strip, strip))
        main, *got = call(
            functools.partial(main_kernel, part, bool(making)),
            (rim,) + outs + making,
            [SMEM] + [VMEM] * 7,
            [pltpu.VMEM((4, 8 * TILE, TILE), BF16)],
            name="main",
            flops=4 * 10**9,
        )(meta, ct, uv if making else ready[1], field, left, right, other, inv)
        if making:
            got, ready = got[:-3], got[-3:]
        cw, rt, edge = ready
        done = call(
            functools.partial(edge_kernel, part),
            outs,
            [SMEM] + [VMEM] * (7 + len(outs)),
            [pltpu.VMEM((PACK, 2 * TILE, TILE), BF16)],
            name="edge",
            flops=2 * 10**9,
        )(meta, cw, edge, main, top, bot, other, inv, *got)
        return done, (ct, inv, cw, rt, edge)

    current = estimate
    ends = ends_of(field, left, right)
    first_end, last_end, profile, uv = lax.optimization_barrier((*ends, illumination.transpose(0, 2, 1), uv))
    ends = [first_end, last_end]
    profiles = gathered(profile, "row")
    forward = (*bands(0, uv), jnp.zeros((groups, TILE, PACK), F32))
    backward = None
    for step in range(ITERS):
        last = step == ITERS - 1
        (ratio, *strips), forward = blur(0, False, forward, field, left, right, ends, observed)
        left, right = exchanged(*strips)
        ends = ends_of(ratio, left, right)
        if backward is None:
            backward = bands(1, lax.optimization_barrier((uv, strips[0]))[0])
        (current, *rest), backward = blur(1, last, backward, ratio, left, right, ends, current)
        if not last:
            field, (left, right) = rest[0], exchanged(*rest[1:])
            ends = ends_of(field, left, right)
    return current


def solution(mesh):
    placed = (
        P(None, "row", "col"),
        P(None, "row", "col"),
        P(("row", "col"), None, None, None, None),
        P("row", "col", None, None),
        P("row", "col", None, None),
        P(None, "row", "col"),
    )
    return jax.shard_map(
        shards, mesh=mesh, in_specs=placed, out_specs=P(None, "row", "col"), check_vma=False
    )
```

```python
import functools

import jax
import jax.numpy as jnp
import numpy as np
from jax import lax
from jax.experimental import pallas as pl
from jax.experimental.pallas import tpu as pltpu
from jax.sharding import PartitionSpec as P

ITERS = 2
F32 = jnp.float32
BF16 = jnp.bfloat16
HIGHEST = lax.Precision.HIGHEST
VMEM = pl.BlockSpec(memory_space=pltpu.VMEM)
SMEM = pl.BlockSpec(memory_space=pltpu.SMEM)

TILE = 128
HALO = 16
PACK = TILE // HALO
TAP_ROWS = 48


def lanes(shape):
    return lax.broadcasted_iota(jnp.int32, shape, len(shape) - 1)


def sublanes(shape):
    return lax.broadcasted_iota(jnp.int32, shape, len(shape) - 2)


def call(body, outs, specs, scratch=(), name=None, flops=0, mib=16):
    return pl.pallas_call(
        body,
        out_shape=outs,
        in_specs=specs,
        out_specs=jax.tree.map(lambda _: VMEM, outs),
        scratch_shapes=list(scratch),
        compiler_params=pltpu.CompilerParams(vmem_limit_bytes=mib * 1024 * 1024),
        cost_estimate=pl.CostEstimate(flops=flops, bytes_accessed=1 << 20, transcendentals=0),
        name=name,
    )


def shift(cells, axis, by):
    count = lax.axis_size(axis)
    return lax.ppermute(cells, axis, [(i, (i + by) % count) for i in range(count)])


def swap(cells, axis, pairs):
    return lax.ppermute(cells, axis, pairs + [(j, i) for i, j in pairs])


def swap_pairs(cells, axis):
    return swap(cells, axis, [(i, i + 1) for i in range(0, lax.axis_size(axis), 2)])


def bank_kernel(bank_ref, out_ref):
    rows, taps = bank_ref.shape
    for block in range(rows // TILE):
        part = bank_ref[block * TILE : (block + 1) * TILE, :]
        part = jnp.concatenate([part, jnp.zeros((TILE, TILE - taps), F32)], axis=1)
        out_ref[:, block * TILE : (block + 1) * TILE] = part.T[:TAP_ROWS].astype(BF16)


def pick_kernel(cols, meta_ref, mine_ref, other_ref, *refs):
    pieces, outs = refs[:-2], refs[-2:]
    zones = pieces[0].shape[1] // TILE
    for keys_ref, out_ref in zip((mine_ref, other_ref), outs):
        ids = (keys_ref[...] + 0.5).astype(jnp.int32)
        for k in range(out_ref.shape[0]):
            got = jnp.zeros((TAP_ROWS, TILE), F32)
            for s, piece in enumerate(pieces):
                first = lax.rem(meta_ref[5] + cols - 2 * s, cols) * zones
                for m in range(zones):
                    got = jnp.where(
                        ids[k : k + 1] == first + m, piece[:, m * TILE : (m + 1) * TILE].astype(F32), got
                    )
            out_ref[k] = got.astype(BF16)


def taps_kernel(taps, keys_ref, mine_ref, other_ref, uv_ref):
    blended = mine_ref.shape[0]
    lane = lanes((1, TILE))
    is_row = (lane & 7) < 4
    picked = []
    total = jnp.zeros((1, TILE), F32)
    mix = keys_ref[blended:, :]
    for k in range(blended):
        got = mine_ref[k].astype(F32) + other_ref[k].astype(F32)
        sums = jnp.sum(got, axis=0, keepdims=True)
        both = sums * pltpu.roll(sums, TILE - 4, 1)
        total = total + jnp.where(is_row, both * mix[k : k + 1], 0.0)
        picked.append(got)
    group = (lanes((TILE, TILE)) >> 3) == (sublanes((TILE, TILE)) >> 3)
    total = jnp.dot(
        jnp.broadcast_to(total, (8, TILE)),
        group.astype(F32),
        precision=HIGHEST,
        preferred_element_type=F32,
    )[:1]
    tap = sublanes((TAP_ROWS, 2 * TILE))
    at = lanes((TAP_ROWS, 2 * TILE))
    half = taps // 2
    goes = jnp.where(at < TILE, (tap - half) & (TILE - 1), TILE + ((half - tap) & (TILE - 1)))
    place = ((goes == at) & (tap < taps)).astype(F32).astype(BF16)
    for k in range(blended):
        got = picked[k]
        scaled = mix[k : k + 1] * got / total
        chosen = jnp.where(is_row, scaled, got).astype(BF16)
        uv_ref[k] = lax.dot_general(
            chosen, place, (((0,), (0,)), ((), ())), preferred_element_type=F32
        ).reshape(uv_ref.shape[1:])


def turned(uv_ref, z, k, r, part, rows, by):
    line = uv_ref[k, z, r : r + 1, part * TILE : (part + 1) * TILE]
    return pltpu.roll(
        jnp.broadcast_to(line, (rows, TILE)), by % TILE, 1, stride=1, stride_axis=0
    )


def bands_kernel(part, rows, meta_ref, uv_ref, *refs):
    *refs, shifts_ref = refs
    if part == 0:
        (ct_ref,) = refs
    else:
        inverse_ref, illum, (ct_ref, inv_ref) = refs[0], refs[1 : 1 + rows], refs[1 + rows :]
        coarse = inverse_ref.shape[1] // rows
        smooth = jnp.zeros((TILE, illum[0].shape[1]), F32)
        for s in range(rows):
            first = pl.multiple_of(lax.rem(meta_ref[4] + rows - s, rows) * coarse, coarse)
            profile = sum(illum[s][n].astype(F32) for n in range(3))
            smooth = smooth + lax.dot_general(
                inverse_ref[meta_ref[4], pl.ds(first, coarse), :],
                profile.T[:coarse],
                (((0,), (0,)), ((), ())),
                precision=HIGHEST,
                preferred_element_type=F32,
            )
        inv = 1.0 / smooth
        for g in range(inv_ref.shape[0]):
            inv_ref[g] = inv[:, g * PACK : (g + 1) * PACK]
    start_shifts(shifts_ref)
    ct_ref[:, TILE:, :] = jnp.zeros((ct_ref.shape[0], TILE, 8 * TILE), BF16)

    def group(g8, carry):
        for i in range(PACK):
            column_bands(part, uv_ref, shifts_ref, g8 * PACK + i, i, ct_ref)
        return carry

    lax.fori_loop(0, ct_ref.shape[0] // PACK, group, 0)


def start_shifts(shifts_ref):
    for t in range(PACK):
        to = (sublanes((TILE, TILE)) + t * HALO) & (TILE - 1)
        shifts_ref[:, t * TILE : (t + 1) * TILE] = (to == lanes((TILE, TILE))).astype(F32).astype(BF16)


def column_bands(part, uv_ref, shifts_ref, z, i, ct_ref):
    low_all = lanes((TILE, TILE)) < TILE // 2
    none = jnp.zeros((TILE, TILE), BF16)
    left, right = TILE + i * HALO, TILE + (i + 4) % PACK * HALO
    base = [turned(uv_ref, z, j // 4, 4 + j % 4, 1 - part, HALO, 0) for j in range(8)]
    base = jnp.concatenate(base, axis=0).astype(BF16)
    for t in range(0, PACK, 2):
        got = jnp.dot(
            base, shifts_ref[:, t * TILE : (t + 2) * TILE], preferred_element_type=F32
        ).astype(BF16)
        first, second = got[:, :TILE], got[:, TILE:]
        if t == 0:
            first, after = jnp.where(low_all, first, none), jnp.where(low_all, none, first)
        elif t == PACK - 2:
            second, before = jnp.where(low_all, none, second), jnp.where(low_all, second, none)
        for j in range(8):
            here, rows = slice(j * TILE, (j + 1) * TILE), slice(j * HALO, (j + 1) * HALO)
            ct_ref[z, t * HALO : (t + 1) * HALO, here] = first[rows]
            ct_ref[z, (t + 1) * HALO : (t + 2) * HALO, here] = second[rows]
            if t == 0:
                ct_ref[z, right : right + HALO, here] = after[rows]
            elif t == PACK - 2:
                ct_ref[z, left : left + HALO, here] = before[rows]


def other_bands(part, uv_ref, ct_ref, z, i, cw_ref, rt_ref, edge_ref):
    low = lanes((HALO, TILE)) < TILE // 2
    lane = lanes((HALO, TILE)) >> 4
    none = jnp.zeros((HALO, TILE), F32)
    above, below = [none] * 2, [none] * 2
    for j in range(8):
        here = slice(j * TILE, (j + 1) * TILE)
        full = turned(uv_ref, z, j // 4, j % 4, part, TILE, 0)
        first, last = full[:HALO], full[TILE - HALO :]
        rt_ref[z, :HALO, here] = jnp.where(low, first, none).astype(BF16)
        rt_ref[z, HALO : TILE - HALO, here] = full[HALO : TILE - HALO].astype(BF16)
        rt_ref[z, TILE - HALO :, here] = jnp.where(low, none, last).astype(BF16)
        spot = (j % 4) * 2
        above[j // 4] = jnp.where(lane == spot, full[(spot + 1) * HALO : (spot + 2) * HALO], above[j // 4])
        below[j // 4] = jnp.where(lane == spot + 1, full[spot * HALO : (spot + 1) * HALO], below[j // 4])
    edge_ref[z] = jnp.concatenate(
        [jnp.concatenate(above, axis=1), jnp.concatenate(below, axis=1)], axis=0
    ).astype(BF16)
    before, after = TILE + i * HALO, TILE + (i + 4) % PACK * HALO
    cw_ref[z, TILE - 2 * HALO :, :] = jnp.zeros((2 * HALO, 4 * TILE), BF16)
    for j in range(0, 8, 2):
        this, other = slice(j * TILE, (j + 1) * TILE), slice((j + 1) * TILE, (j + 2) * TILE)
        for t in range(6):
            a = before if t == 0 else (t - 1) * HALO
            b = after if t == 5 else (t + 3) * HALO
            cw_ref[z, t * HALO : (t + 1) * HALO, j * TILE // 2 : j * TILE // 2 + TILE] = jnp.where(
                low, ct_ref[z, a : a + HALO, this], ct_ref[z, b : b + HALO, other]
            )


def sides_of(left, right, meta_ref):
    left = jnp.where(meta_ref[0] > 0, left, jnp.zeros_like(left))
    right = jnp.where(meta_ref[1] > 0, right, jnp.zeros_like(right))
    return left, right


def joined(left, right, parity):
    low = lanes(left.shape) < TILE // 2
    return jnp.where(low, left, right) if parity == 0 else jnp.where(low, right, left)


def windows(field, left, right, i):
    lane = lanes(field.shape)
    left = pltpu.roll(left, -i * HALO % TILE, 1)
    right = pltpu.roll(right, (80 - (i + 4) % PACK * HALO) % TILE, 1)
    first = jnp.where(lane < HALO, left, pltpu.roll(field, HALO, 1))
    second = jnp.where(lane < 80, pltpu.roll(field, 80, 1), right)
    return first, second


def column_pass(wide, cw_ref, z, q_ref, slot):
    rows = wide.shape[0] // 2
    low = lanes((rows, TILE)) < TILE // 2
    for n in range(2):
        got = jnp.dot(
            wide, cw_ref[z, :, n * 256 : (n + 1) * 256], preferred_element_type=F32
        ).astype(BF16)
        for p in range(2):
            first, second = got[:rows, p * TILE : (p + 1) * TILE], got[rows:, p * TILE : (p + 1) * TILE]
            at = (n * 4 + p * 2) * rows
            q_ref[slot, at : at + rows, :] = jnp.where(low, first, pltpu.roll(second, TILE // 2, 1))
            q_ref[slot, at + rows : at + 2 * rows, :] = jnp.where(low, pltpu.roll(first, TILE // 2, 1), second)


def pack_strips(value, i, g8, rows, right_ref, left_ref):
    lane = lanes(value.shape) >> 4
    at = (i + 4) % PACK
    to_right = pltpu.roll(value, (i * HALO - 112) % TILE, 1)
    to_left = pltpu.roll(value, at * HALO, 1)
    if i == 0:
        right_ref[g8, rows] = to_right
        left_ref[g8, rows] = to_left
    else:
        right_ref[g8, rows] = jnp.where(lane == i, to_right, right_ref[g8, rows])
        left_ref[g8, rows] = jnp.where(lane == at, to_left, left_ref[g8, rows])


def finish(part, blurred, g8, i, rows, a_ref, inv_ref, outs):
    z = g8 * PACK + i
    if part == 0:
        value = a_ref[z, rows] / blurred
    else:
        value = a_ref[z, rows] * blurred * inv_ref[g8, rows, i : i + 1]
        outs[0][z, rows] = value
        outs = outs[1:]
    if outs:
        b_ref, right_ref, left_ref = outs
        value = value.astype(BF16)
        b_ref[z, rows] = value
        pack_strips(value, i, g8, rows, right_ref, left_ref)


def main_kernel(part, making, meta_ref, ct_ref, rt_ref, field_ref, left_ref, right_ref, a_ref, inv_ref, rim_ref, *refs):
    outs, q_ref = refs[:-1], refs[-1]
    if making:
        outs, made, uv_ref, rt_ref = outs[:-3], outs[-3:], rt_ref, outs[-2]
    if making == 2:
        shifts_ref, q_ref = refs[-1], refs[-2]
        *outs, ct_ref, cw_ref, rt_ref, edge_ref = refs[:-2]
        made = cw_ref, rt_ref, edge_ref
        start_shifts(shifts_ref)
        for z in range(ct_ref.shape[0]):
            for t in range(PACK):
                if t % 4 != z % 4:
                    ct_ref[z, TILE + t * HALO : TILE + (t + 1) * HALO, :] = jnp.zeros((HALO, 8 * TILE), BF16)
    inner = slice(HALO, TILE - HALO)

    def group(g8, carry):
        sides = sides_of(left_ref[g8], right_ref[g8], meta_ref)
        halos = [joined(*sides, parity) for parity in range(2)]

        def columns(i):
            wide = jnp.concatenate([field_ref[g8 * PACK + i], halos[i // 4]], axis=1)
            for n in range(4):
                got = jnp.dot(
                    wide, ct_ref[g8 * PACK + i, :, n * 256 : (n + 1) * 256], preferred_element_type=F32
                ).astype(BF16)
                q_ref[i % 4, n * 256 : n * 256 + TILE, :] = got[:, :TILE]
                q_ref[i % 4, n * 256 + TILE : (n + 1) * 256, :] = got[:, TILE:]

        def rows(i):
            z = g8 * PACK + i
            blurred = jnp.dot(rt_ref[z], q_ref[i % 4], preferred_element_type=F32)
            rim_ref[z, :HALO] = blurred[:HALO]
            rim_ref[z, HALO:] = blurred[TILE - HALO :]
            finish(part, blurred[inner], g8, i, inner, a_ref, inv_ref, outs)

        def bands(i):
            if making == 2:
                column_bands(part, uv_ref, shifts_ref, g8 * PACK + i, i, ct_ref)
            if making:
                other_bands(part, uv_ref, ct_ref, g8 * PACK + i, i, *made)

        bands(0)
        bands(1)
        columns(0)
        bands(2)
        columns(1)
        for i in range(PACK):
            if i + 3 < PACK:
                bands(i + 3)
            if i + 2 < PACK:
                columns(i + 2)
            rows(i)
        return carry

    for g8 in range(field_ref.shape[0] // PACK):
        group(g8, 0)


def edge_kernel(part, meta_ref, cw_ref, edge_ref, rim_ref, top_ref, bot_ref, a_ref, inv_ref, *refs):
    count = len(refs) // 2
    made, outs, q_ref = refs[:count], refs[count:-1], refs[-1]
    depth = rim_ref.shape[0]
    inner = slice(HALO, TILE - HALO)

    def group(g8, carry):
        halos = [sides_of(ref[depth + g8], ref[depth + 2 + g8], meta_ref) for ref in (top_ref, bot_ref)]
        for old, new in zip(made, outs):
            each = pl.ds(g8 * (new.shape[0] // (depth // PACK)), new.shape[0] // (depth // PACK))
            new[each, inner] = old[each, inner]

        def columns(i):
            z = g8 * PACK + i
            pairs = []
            for s, ref in enumerate((top_ref, bot_ref)):
                both = windows(ref[z], *halos[s], i)
                pairs.append([jnp.where(meta_ref[2 + s] > 0, w, jnp.zeros_like(w)) for w in both])
            wide = jnp.concatenate([pairs[0][0], pairs[1][0], pairs[0][1], pairs[1][1]], axis=0)
            column_pass(wide, cw_ref, z, q_ref, i)

        def rows(i):
            z = g8 * PACK + i
            blurred = rim_ref[z] + jnp.dot(edge_ref[z], q_ref[i], preferred_element_type=F32)
            for s, at in enumerate((slice(0, HALO), slice(TILE - HALO, TILE))):
                finish(part, blurred[s * HALO : (s + 1) * HALO], g8, i, at, a_ref, inv_ref, outs)

        for i in range(PACK):
            columns(i)
        for i in range(PACK):
            rows(i)
        return carry

    for g8 in range(depth // PACK):
        group(g8, 0)


def keys_kernel(ids_ref, mix_ref, illum_ref, keys_ref, plane_ref):
    spread = (lanes((ids_ref.shape[1], TILE)) >> 3 == sublanes((ids_ref.shape[1], TILE))).astype(F32)
    both = jnp.concatenate([ids_ref[...].astype(F32), mix_ref[...]], axis=0)
    keys_ref[...] = jnp.dot(both, spread, precision=HIGHEST, preferred_element_type=F32)
    rest = illum_ref[:, 0, :]
    depth, coarse = rest.shape
    parts = []
    for _ in range(3):
        part = rest.astype(BF16)
        rest = rest - part.astype(F32)
        parts.append(jnp.concatenate([part, jnp.zeros((depth, TILE - coarse), BF16)], axis=1))
    for n in range(3):
        plane_ref[n] = parts[n]


def first_kernel(est_ref, b_ref, right_ref, left_ref):
    def group(g8, carry):
        for i in range(PACK):
            value = est_ref[g8 * PACK + i].astype(BF16)
            b_ref[g8 * PACK + i] = value
            pack_strips(value, i, g8, slice(0, TILE), right_ref, left_ref)
        return carry

    lax.fori_loop(0, est_ref.shape[0] // PACK, group, 0)


def smoothing(length, rows):
    stiffness = float(length * length) / 16.0
    d = np.diff(np.eye(length), axis=0)
    inverse = np.linalg.inv(np.eye(length) + stiffness * d.T @ d)
    wide = np.repeat(inverse, TILE * rows // length, axis=0)
    return jnp.asarray(wide.reshape(rows, TILE, length).transpose(0, 2, 1), F32)


def shards(observed, estimate, psf_bank, zone_ids, mix_weights, illumination):
    depth = estimate.shape[0]
    zones_here, _, _, rank, taps = psf_bank.shape
    n_row, n_col = lax.axis_size("row"), lax.axis_size("col")
    row, col = lax.axis_index("row"), lax.axis_index("col")
    groups = depth // PACK
    flag = lambda x: x.astype(jnp.int32)
    meta = jnp.stack(
        [flag(col > 0), flag(col < n_col - 1), flag(row > 0), flag(row < n_row - 1), flag(row), flag(col)]
    )
    volume = jax.ShapeDtypeStruct((depth, TILE, TILE), F32)
    narrow = jax.ShapeDtypeStruct((depth, TILE, TILE), BF16)
    strip = jax.ShapeDtypeStruct((groups, TILE, TILE), BF16)


    def ends_of(field, left, right, *more):
        return [
            jnp.concatenate([field[:, rows], left[:, rows], right[:, rows], *more], axis=0)
            for rows in (slice(0, HALO), slice(TILE - HALO, TILE))
        ]

    def exchanged(to_right, to_left):
        return shift(to_right, "col", 1), shift(to_left, "col", -1)

    blended = zone_ids.shape[-1]
    flat = (zones_here * depth * 2 * rank, taps)
    bank = call(
        bank_kernel,
        jax.ShapeDtypeStruct((TAP_ROWS, zones_here * TILE), BF16),
        [VMEM],
        name="bank",
        flops=4 * 10**9,
    )(psf_bank.reshape(flat))
    pieces = [bank] + [shift(bank, "col", s) for s in range(2, n_col, 2)]
    field, to_right, to_left = call(
        first_kernel, (narrow, strip, strip), [VMEM], name="first", flops=10**9
    )(estimate)
    keys, plane = call(
        keys_kernel,
        (jax.ShapeDtypeStruct((2 * blended, TILE), F32), jax.ShapeDtypeStruct((3, depth, TILE), BF16)),
        [VMEM] * 3,
        name="keys",
    )(zone_ids[0, 0].T, mix_weights[0, 0].T, illumination.transpose(0, 2, 1))
    other_keys = swap_pairs(keys, "col")
    left, right = exchanged(to_right, to_left)
    inverse = smoothing(illumination.shape[1] * n_row, n_row)
    factors = jax.ShapeDtypeStruct((blended, TAP_ROWS, TILE), BF16)
    mine, others = call(
        functools.partial(pick_kernel, n_col),
        (factors, factors),
        [SMEM] + [VMEM] * (2 + len(pieces)),
        name="pick",
    )(meta, keys, other_keys, *pieces)
    ends = ends_of(field, left, right, plane)
    uv = call(
        functools.partial(taps_kernel, taps),
        jax.ShapeDtypeStruct((blended, depth, 2 * rank, 2 * TILE), F32),
        [VMEM] * 3,
        name="taps",
    )(keys, mine, swap_pairs(others, "col"))

    shape = lambda *s: jax.ShapeDtypeStruct((depth,) + s, BF16)

    def bands(part, uv, *profiles):
        outs = (shape(2 * TILE, 8 * TILE),)
        args = [meta, uv]
        if part == 1:
            outs = outs + (jax.ShapeDtypeStruct((groups, TILE, PACK), F32),)
            args = [*args, inverse, *profiles]
        return call(
            functools.partial(bands_kernel, part, n_row),
            outs,
            [SMEM] + [VMEM] * (len(args) - 1),
            [pltpu.VMEM((TILE, 8 * TILE), BF16)],
            name="bands",
            flops=4 * 10**9,
        )(*args)

    def blur(part, last, made, field, left, right, ends, other):
        ct, inv, *ready = made
        making = () if ready else (shape(TILE, 4 * TILE), shape(TILE, 8 * TILE), shape(2 * HALO, 2 * TILE))
        making = making if ct is not None else (shape(2 * TILE, 8 * TILE), *making)
        scratch = [pltpu.VMEM((4, 8 * TILE, TILE), BF16)]
        bot, top = shift(ends[0], "row", -1), shift(ends[1], "row", 1)
        rim = jax.ShapeDtypeStruct((depth, 2 * HALO, TILE), F32)
        outs = ((volume,) if part == 1 else ()) + (() if last else (narrow, strip, strip))
        main, *got = call(
            functools.partial(main_kernel, part, len(making) - 2 if making else 0),
            (rim,) + outs + making,
            [SMEM] + [VMEM] * 7,
            scratch if ct is not None else scratch + [pltpu.VMEM((TILE, 8 * TILE), BF16)],
            name="main",
            flops=4 * 10**9,
        )(meta, uv if ct is None else ct, uv if making else ready[1], field, left, right, other, inv)
        if making:
            got, ready = got[:-3], got[-3:]
        if ct is None:
            *got, ct = got
        cw, rt, edge = ready
        done = call(
            functools.partial(edge_kernel, part),
            outs,
            [SMEM] + [VMEM] * (7 + len(outs)),
            [pltpu.VMEM((PACK, 2 * TILE, TILE), BF16)],
            name="edge",
            flops=2 * 10**9,
        )(meta, cw, edge, main, top, bot, other, inv, *got)
        return done, (ct, inv, cw, rt, edge), (top, bot)

    current = estimate
    far = [shift(plane, "row", s) for s in range(2, n_row - 1)]
    forward = (None, jnp.zeros((groups, TILE, PACK), F32))
    backward = None
    for step in range(ITERS):
        last = step == ITERS - 1
        (ratio, *strips), forward, ends = blur(0, False, forward, field, left, right, ends, observed)
        left, right = exchanged(*strips)
        if backward is None:
            above, below = (end[-3:] for end in ends)
            backward = bands(1, lax.optimization_barrier((uv, strips[0]))[0], plane, above, *far, below)
        ends = ends_of(ratio, left, right)
        (current, *rest), backward, _ = blur(1, last, backward, ratio, left, right, ends, current)
        if not last:
            field, (left, right) = rest[0], exchanged(*rest[1:])
            ends = ends_of(field, left, right)
    return current


def solution(mesh):
    placed = (
        P(None, "row", "col"),
        P(None, "row", "col"),
        P(("row", "col"), None, None, None, None),
        P("row", "col", None, None),
        P("row", "col", None, None),
        P(None, "row", "col"),
    )
    return jax.shard_map(
        shards, mesh=mesh, in_specs=placed, out_specs=P(None, "row", "col"), check_vma=False
    )
```

```python
import functools

import jax
import jax.numpy as jnp
import numpy as np
from jax import lax
from jax.experimental import pallas as pl
from jax.experimental.pallas import tpu as pltpu
from jax.sharding import PartitionSpec as P

ITERS = 2
F32 = jnp.float32
BF16 = jnp.bfloat16
HIGHEST = lax.Precision.HIGHEST
VMEM = pl.BlockSpec(memory_space=pltpu.VMEM)
SMEM = pl.BlockSpec(memory_space=pltpu.SMEM)

TILE = 128
HALO = 16
PACK = TILE // HALO
TAP_ROWS = 48


def lanes(shape):
    return lax.broadcasted_iota(jnp.int32, shape, len(shape) - 1)


def sublanes(shape):
    return lax.broadcasted_iota(jnp.int32, shape, len(shape) - 2)


def call(body, outs, specs, scratch=(), name=None, flops=0, mib=16):
    return pl.pallas_call(
        body,
        out_shape=outs,
        in_specs=specs,
        out_specs=jax.tree.map(lambda _: VMEM, outs),
        scratch_shapes=list(scratch),
        compiler_params=pltpu.CompilerParams(vmem_limit_bytes=mib * 1024 * 1024),
        cost_estimate=pl.CostEstimate(flops=flops, bytes_accessed=1 << 20, transcendentals=0),
        name=name,
    )


def shift(cells, axis, by):
    count = lax.axis_size(axis)
    return lax.ppermute(cells, axis, [(i, (i + by) % count) for i in range(count)])


def swap(cells, axis, pairs):
    return lax.ppermute(cells, axis, pairs + [(j, i) for i, j in pairs])


def swap_pairs(cells, axis):
    return swap(cells, axis, [(i, i + 1) for i in range(0, lax.axis_size(axis), 2)])


def outer_columns(rows, cols):
    pairs = []
    for r in range(rows):
        for c in range(cols):
            to = c - 1 if c % 2 == 0 else c + 1
            pairs.append((r * cols + c, r * cols + to if 0 <= to < cols else (r ^ 1) * cols + c))
    return pairs


def outer_rows(rows, cols):
    pairs = []
    for r in range(rows):
        for c in range(cols):
            to = r - 1 if r % 2 == 0 else r + 1
            pairs.append((r * cols + c, to * cols + c if 0 <= to < rows else r * cols + (c ^ 1)))
    return pairs


def bank_kernel(bank_ref, out_ref):
    rows, taps = bank_ref.shape
    for block in range(rows // TILE):
        part = bank_ref[block * TILE : (block + 1) * TILE, :]
        part = jnp.concatenate([part, jnp.zeros((TILE, TILE - taps), F32)], axis=1)
        out_ref[:, block * TILE : (block + 1) * TILE] = part.T[:TAP_ROWS].astype(BF16)


def pick_kernel(cols, meta_ref, mine_ref, other_ref, *refs):
    pieces, outs = refs[:-2], refs[-2:]
    zones = pieces[0].shape[1] // TILE
    for keys_ref, out_ref in zip((mine_ref, other_ref), outs):
        ids = (keys_ref[...] + 0.5).astype(jnp.int32)
        for k in range(out_ref.shape[0]):
            got = jnp.zeros((TAP_ROWS, TILE), F32)
            for s, piece in enumerate(pieces):
                first = (meta_ref[5] ^ (2 * s)) * zones
                for m in range(zones):
                    got = jnp.where(
                        ids[k : k + 1] == first + m, piece[:, m * TILE : (m + 1) * TILE].astype(F32), got
                    )
            out_ref[k] = got.astype(BF16)


def taps_kernel(taps, keys_ref, mine_ref, other_ref, uv_ref):
    blended = mine_ref.shape[0]
    lane = lanes((1, TILE))
    is_row = (lane & 7) < 4
    picked = []
    total = jnp.zeros((1, TILE), F32)
    mix = keys_ref[blended:, :]
    for k in range(blended):
        got = mine_ref[k].astype(F32) + other_ref[k].astype(F32)
        sums = jnp.sum(got, axis=0, keepdims=True)
        both = sums * pltpu.roll(sums, TILE - 4, 1)
        total = total + jnp.where(is_row, both * mix[k : k + 1], 0.0)
        picked.append(got)
    group = (lanes((TILE, TILE)) >> 3) == (sublanes((TILE, TILE)) >> 3)
    total = jnp.dot(
        jnp.broadcast_to(total, (8, TILE)),
        group.astype(F32),
        precision=HIGHEST,
        preferred_element_type=F32,
    )[:1]
    tap = sublanes((TAP_ROWS, 2 * TILE))
    at = lanes((TAP_ROWS, 2 * TILE))
    half = taps // 2
    goes = jnp.where(at < TILE, (tap - half) & (TILE - 1), TILE + ((half - tap) & (TILE - 1)))
    place = ((goes == at) & (tap < taps)).astype(F32).astype(BF16)
    for k in range(blended):
        got = picked[k]
        scaled = mix[k : k + 1] * got / total
        chosen = jnp.where(is_row, scaled, got).astype(BF16)
        uv_ref[k] = lax.dot_general(
            chosen, place, (((0,), (0,)), ((), ())), preferred_element_type=F32
        ).reshape(uv_ref.shape[1:])


def turned(uv_ref, z, k, r, part, rows, by):
    line = uv_ref[k, z, r : r + 1, part * TILE : (part + 1) * TILE]
    return pltpu.roll(
        jnp.broadcast_to(line, (rows, TILE)), by % TILE, 1, stride=1, stride_axis=0
    )


def bands_kernel(part, rows, meta_ref, uv_ref, *refs):
    *refs, shifts_ref = refs
    if part == 0:
        (ct_ref,) = refs
    else:
        inverse_ref, illum, (ct_ref, inv_ref) = refs[0], refs[1 : 1 + rows], refs[1 + rows :]
        coarse = inverse_ref.shape[1] // rows
        smooth = jnp.zeros((TILE, illum[0].shape[1]), F32)
        for s in range(rows):
            first = pl.multiple_of((meta_ref[4] ^ s) * coarse, coarse)
            profile = sum(illum[s][n].astype(F32) for n in range(3))
            smooth = smooth + lax.dot_general(
                inverse_ref[meta_ref[4], pl.ds(first, coarse), :],
                profile.T[:coarse],
                (((0,), (0,)), ((), ())),
                precision=HIGHEST,
                preferred_element_type=F32,
            )
        inv = 1.0 / smooth
        for g in range(inv_ref.shape[0]):
            inv_ref[g] = inv[:, g * PACK : (g + 1) * PACK]
    start_shifts(shifts_ref)
    ct_ref[:, TILE:, :] = jnp.zeros((ct_ref.shape[0], TILE, 8 * TILE), BF16)

    def group(g8, carry):
        for i in range(PACK):
            column_bands(part, uv_ref, shifts_ref, g8 * PACK + i, i, ct_ref)
        return carry

    lax.fori_loop(0, ct_ref.shape[0] // PACK, group, 0)


def start_shifts(shifts_ref):
    for t in range(PACK):
        to = (sublanes((TILE, TILE)) + t * HALO) & (TILE - 1)
        shifts_ref[:, t * TILE : (t + 1) * TILE] = (to == lanes((TILE, TILE))).astype(F32).astype(BF16)


def column_bands(part, uv_ref, shifts_ref, z, i, ct_ref):
    low_all = lanes((TILE, TILE)) < TILE // 2
    none = jnp.zeros((TILE, TILE), BF16)
    left, right = TILE + i * HALO, TILE + (i + 4) % PACK * HALO
    base = [turned(uv_ref, z, j // 4, 4 + j % 4, 1 - part, HALO, 0) for j in range(8)]
    base = jnp.concatenate(base, axis=0).astype(BF16)
    for t in range(0, PACK, 2):
        got = jnp.dot(
            base, shifts_ref[:, t * TILE : (t + 2) * TILE], preferred_element_type=F32
        ).astype(BF16)
        first, second = got[:, :TILE], got[:, TILE:]
        if t == 0:
            first, after = jnp.where(low_all, first, none), jnp.where(low_all, none, first)
        elif t == PACK - 2:
            second, before = jnp.where(low_all, none, second), jnp.where(low_all, second, none)
        for j in range(8):
            here, rows = slice(j * TILE, (j + 1) * TILE), slice(j * HALO, (j + 1) * HALO)
            ct_ref[z, t * HALO : (t + 1) * HALO, here] = first[rows]
            ct_ref[z, (t + 1) * HALO : (t + 2) * HALO, here] = second[rows]
            if t == 0:
                ct_ref[z, right : right + HALO, here] = after[rows]
            elif t == PACK - 2:
                ct_ref[z, left : left + HALO, here] = before[rows]


def other_bands(part, uv_ref, ct_ref, z, i, cw_ref, rt_ref, edge_ref):
    low = lanes((HALO, TILE)) < TILE // 2
    lane = lanes((HALO, TILE)) >> 4
    none = jnp.zeros((HALO, TILE), F32)
    above, below = [none] * 2, [none] * 2
    for j in range(8):
        here = slice(j * TILE, (j + 1) * TILE)
        full = turned(uv_ref, z, j // 4, j % 4, part, TILE, 0)
        first, last = full[:HALO], full[TILE - HALO :]
        rt_ref[z, :HALO, here] = jnp.where(low, first, none).astype(BF16)
        rt_ref[z, HALO : TILE - HALO, here] = full[HALO : TILE - HALO].astype(BF16)
        rt_ref[z, TILE - HALO :, here] = jnp.where(low, none, last).astype(BF16)
        spot = (j % 4) * 2
        above[j // 4] = jnp.where(lane == spot, full[(spot + 1) * HALO : (spot + 2) * HALO], above[j // 4])
        below[j // 4] = jnp.where(lane == spot + 1, full[spot * HALO : (spot + 1) * HALO], below[j // 4])
    edge_ref[z] = jnp.concatenate(
        [jnp.concatenate(above, axis=1), jnp.concatenate(below, axis=1)], axis=0
    ).astype(BF16)
    before, after = TILE + i * HALO, TILE + (i + 4) % PACK * HALO
    cw_ref[z, TILE - 2 * HALO :, :] = jnp.zeros((2 * HALO, 4 * TILE), BF16)
    for j in range(0, 8, 2):
        this, other = slice(j * TILE, (j + 1) * TILE), slice((j + 1) * TILE, (j + 2) * TILE)
        for t in range(6):
            a = before if t == 0 else (t - 1) * HALO
            b = after if t == 5 else (t + 3) * HALO
            cw_ref[z, t * HALO : (t + 1) * HALO, j * TILE // 2 : j * TILE // 2 + TILE] = jnp.where(
                low, ct_ref[z, a : a + HALO, this], ct_ref[z, b : b + HALO, other]
            )


def sides_of(left, right, meta_ref):
    left = jnp.where(meta_ref[0] > 0, left, jnp.zeros_like(left))
    right = jnp.where(meta_ref[1] > 0, right, jnp.zeros_like(right))
    return left, right


def joined(left, right, parity):
    low = lanes(left.shape) < TILE // 2
    return jnp.where(low, left, right) if parity == 0 else jnp.where(low, right, left)


def windows(field, left, right, i):
    lane = lanes(field.shape)
    left = pltpu.roll(left, -i * HALO % TILE, 1)
    right = pltpu.roll(right, (80 - (i + 4) % PACK * HALO) % TILE, 1)
    first = jnp.where(lane < HALO, left, pltpu.roll(field, HALO, 1))
    second = jnp.where(lane < 80, pltpu.roll(field, 80, 1), right)
    return first, second


def column_pass(wide, cw_ref, z, q_ref, slot):
    rows = wide.shape[0] // 2
    low = lanes((rows, TILE)) < TILE // 2
    for n in range(2):
        got = jnp.dot(
            wide, cw_ref[z, :, n * 256 : (n + 1) * 256], preferred_element_type=F32
        ).astype(BF16)
        for p in range(2):
            first, second = got[:rows, p * TILE : (p + 1) * TILE], got[rows:, p * TILE : (p + 1) * TILE]
            at = (n * 4 + p * 2) * rows
            q_ref[slot, at : at + rows, :] = jnp.where(low, first, pltpu.roll(second, TILE // 2, 1))
            q_ref[slot, at + rows : at + 2 * rows, :] = jnp.where(low, pltpu.roll(first, TILE // 2, 1), second)


def pack_strips(value, i, g8, rows, right_ref, left_ref):
    lane = lanes(value.shape) >> 4
    at = (i + 4) % PACK
    to_right = pltpu.roll(value, (i * HALO - 112) % TILE, 1)
    to_left = pltpu.roll(value, at * HALO, 1)
    if i == 0:
        right_ref[g8, rows] = to_right
        left_ref[g8, rows] = to_left
    else:
        right_ref[g8, rows] = jnp.where(lane == i, to_right, right_ref[g8, rows])
        left_ref[g8, rows] = jnp.where(lane == at, to_left, left_ref[g8, rows])


def finish(part, blurred, g8, i, rows, a_ref, inv_ref, outs):
    z = g8 * PACK + i
    if part == 0:
        value = a_ref[z, rows] / blurred
    else:
        value = a_ref[z, rows] * blurred * inv_ref[g8, rows, i : i + 1]
        outs[0][z, rows] = value
        outs = outs[1:]
    if outs:
        b_ref, right_ref, left_ref = outs
        value = value.astype(BF16)
        b_ref[z, rows] = value
        pack_strips(value, i, g8, rows, right_ref, left_ref)


def main_kernel(part, making, meta_ref, ct_ref, rt_ref, field_ref, left_ref, right_ref, a_ref, inv_ref, rim_ref, *refs):
    outs, q_ref = refs[:-1], refs[-1]
    if making:
        outs, made, uv_ref, rt_ref = outs[:-3], outs[-3:], rt_ref, outs[-2]
    if making == 2:
        shifts_ref, q_ref = refs[-1], refs[-2]
        *outs, ct_ref, cw_ref, rt_ref, edge_ref = refs[:-2]
        made = cw_ref, rt_ref, edge_ref
        start_shifts(shifts_ref)
        for z in range(ct_ref.shape[0]):
            for t in range(PACK):
                if t % 4 != z % 4:
                    ct_ref[z, TILE + t * HALO : TILE + (t + 1) * HALO, :] = jnp.zeros((HALO, 8 * TILE), BF16)
    inner = slice(HALO, TILE - HALO)

    def group(g8, carry):
        sides = sides_of(left_ref[g8], right_ref[g8], meta_ref)
        halos = [joined(*sides, parity) for parity in range(2)]

        def columns(i):
            wide = jnp.concatenate([field_ref[g8 * PACK + i], halos[i // 4]], axis=1)
            for n in range(4):
                got = jnp.dot(
                    wide, ct_ref[g8 * PACK + i, :, n * 256 : (n + 1) * 256], preferred_element_type=F32
                ).astype(BF16)
                q_ref[i % 4, n * 256 : n * 256 + TILE, :] = got[:, :TILE]
                q_ref[i % 4, n * 256 + TILE : (n + 1) * 256, :] = got[:, TILE:]

        def rows(i):
            z = g8 * PACK + i
            blurred = jnp.dot(rt_ref[z], q_ref[i % 4], preferred_element_type=F32)
            rim_ref[z, :HALO] = blurred[:HALO]
            rim_ref[z, HALO:] = blurred[TILE - HALO :]
            finish(part, blurred[inner], g8, i, inner, a_ref, inv_ref, outs)

        def bands(i):
            if making == 2:
                column_bands(part, uv_ref, shifts_ref, g8 * PACK + i, i, ct_ref)
            if making:
                other_bands(part, uv_ref, ct_ref, g8 * PACK + i, i, *made)

        bands(0)
        bands(1)
        columns(0)
        bands(2)
        columns(1)
        for i in range(PACK):
            if i + 3 < PACK:
                bands(i + 3)
            if i + 2 < PACK:
                columns(i + 2)
            rows(i)
        return carry

    for g8 in range(field_ref.shape[0] // PACK):
        group(g8, 0)


def edge_kernel(part, meta_ref, cw_ref, edge_ref, rim_ref, top_ref, bot_ref, a_ref, inv_ref, *refs):
    count = len(refs) // 2
    made, outs, q_ref = refs[:count], refs[count:-1], refs[-1]
    depth = rim_ref.shape[0]
    inner = slice(HALO, TILE - HALO)

    def group(g8, carry):
        halos = [sides_of(ref[depth + g8], ref[depth + 2 + g8], meta_ref) for ref in (top_ref, bot_ref)]
        for old, new in zip(made, outs):
            each = pl.ds(g8 * (new.shape[0] // (depth // PACK)), new.shape[0] // (depth // PACK))
            new[each, inner] = old[each, inner]

        def columns(i):
            z = g8 * PACK + i
            pairs = []
            for s, ref in enumerate((top_ref, bot_ref)):
                both = windows(ref[z], *halos[s], i)
                pairs.append([jnp.where(meta_ref[2 + s] > 0, w, jnp.zeros_like(w)) for w in both])
            wide = jnp.concatenate([pairs[0][0], pairs[1][0], pairs[0][1], pairs[1][1]], axis=0)
            column_pass(wide, cw_ref, z, q_ref, i)

        def rows(i):
            z = g8 * PACK + i
            blurred = rim_ref[z] + jnp.dot(edge_ref[z], q_ref[i], preferred_element_type=F32)
            for s, at in enumerate((slice(0, HALO), slice(TILE - HALO, TILE))):
                finish(part, blurred[s * HALO : (s + 1) * HALO], g8, i, at, a_ref, inv_ref, outs)

        for i in range(PACK):
            columns(i)
        for i in range(PACK):
            rows(i)
        return carry

    for g8 in range(depth // PACK):
        group(g8, 0)


def keys_kernel(ids_ref, mix_ref, illum_ref, keys_ref, plane_ref):
    spread = (lanes((ids_ref.shape[1], TILE)) >> 3 == sublanes((ids_ref.shape[1], TILE))).astype(F32)
    both = jnp.concatenate([ids_ref[...].astype(F32), mix_ref[...]], axis=0)
    keys_ref[...] = jnp.dot(both, spread, precision=HIGHEST, preferred_element_type=F32)
    rest = illum_ref[:, 0, :]
    depth, coarse = rest.shape
    parts = []
    for _ in range(3):
        part = rest.astype(BF16)
        rest = rest - part.astype(F32)
        parts.append(jnp.concatenate([part, jnp.zeros((depth, TILE - coarse), BF16)], axis=1))
    for n in range(3):
        plane_ref[n] = parts[n]


def first_kernel(est_ref, b_ref, right_ref, left_ref):
    def group(g8, carry):
        for i in range(PACK):
            value = est_ref[g8 * PACK + i].astype(BF16)
            b_ref[g8 * PACK + i] = value
            pack_strips(value, i, g8, slice(0, TILE), right_ref, left_ref)
        return carry

    lax.fori_loop(0, est_ref.shape[0] // PACK, group, 0)


def smoothing(length, rows):
    stiffness = float(length * length) / 16.0
    d = np.diff(np.eye(length), axis=0)
    inverse = np.linalg.inv(np.eye(length) + stiffness * d.T @ d)
    wide = np.repeat(inverse, TILE * rows // length, axis=0)
    return jnp.asarray(wide.reshape(rows, TILE, length).transpose(0, 2, 1), F32)


def shards(observed, estimate, psf_bank, zone_ids, mix_weights, illumination):
    depth = estimate.shape[0]
    zones_here, _, _, rank, taps = psf_bank.shape
    n_row, n_col = lax.axis_size("row"), lax.axis_size("col")
    row, col = lax.axis_index("row"), lax.axis_index("col")
    groups = depth // PACK
    flag = lambda x: x.astype(jnp.int32)
    meta = jnp.stack(
        [flag(col > 0), flag(col < n_col - 1), flag(row > 0), flag(row < n_row - 1), flag(row), flag(col)]
    )
    volume = jax.ShapeDtypeStruct((depth, TILE, TILE), F32)
    narrow = jax.ShapeDtypeStruct((depth, TILE, TILE), BF16)
    strip = jax.ShapeDtypeStruct((groups, TILE, TILE), BF16)


    def ends_of(field, left, right, *more):
        return [
            jnp.concatenate([field[:, rows], left[:, rows], right[:, rows], *more], axis=0)
            for rows in (slice(0, HALO), slice(TILE - HALO, TILE))
        ]

    def exchanged(to_right, to_left):
        even = meta[5] % 2 == 0
        near = swap_pairs(jnp.where(even, to_right, to_left), "col")
        far = lax.ppermute(jnp.where(even, to_left, to_right), ("row", "col"), outer_columns(n_row, n_col))
        return jnp.where(even, far, near), jnp.where(even, near, far)

    blended = zone_ids.shape[-1]
    flat = (zones_here * depth * 2 * rank, taps)
    bank = call(
        bank_kernel,
        jax.ShapeDtypeStruct((TAP_ROWS, zones_here * TILE), BF16),
        [VMEM],
        name="bank",
        flops=4 * 10**9,
    )(psf_bank.reshape(flat))
    pieces = [bank] + [lax.ppermute(bank, "col", [(i, i ^ s) for i in range(n_col)]) for s in range(2, n_col, 2)]
    field, to_right, to_left = call(
        first_kernel, (narrow, strip, strip), [VMEM], name="first", flops=10**9
    )(estimate)
    keys, plane = call(
        keys_kernel,
        (jax.ShapeDtypeStruct((2 * blended, TILE), F32), jax.ShapeDtypeStruct((3, depth, TILE), BF16)),
        [VMEM] * 3,
        name="keys",
    )(zone_ids[0, 0].T, mix_weights[0, 0].T, illumination.transpose(0, 2, 1))
    other_keys = swap_pairs(keys, "col")
    left, right = exchanged(to_right, to_left)
    inverse = smoothing(illumination.shape[1] * n_row, n_row)
    factors = jax.ShapeDtypeStruct((blended, TAP_ROWS, TILE), BF16)
    mine, others = call(
        functools.partial(pick_kernel, n_col),
        (factors, factors),
        [SMEM] + [VMEM] * (2 + len(pieces)),
        name="pick",
    )(meta, keys, other_keys, *pieces)
    ends = ends_of(field, left, right, plane)
    uv = call(
        functools.partial(taps_kernel, taps),
        jax.ShapeDtypeStruct((blended, depth, 2 * rank, 2 * TILE), F32),
        [VMEM] * 3,
        name="taps",
    )(keys, mine, swap_pairs(others, "col"))

    shape = lambda *s: jax.ShapeDtypeStruct((depth,) + s, BF16)

    def bands(part, uv, *profiles):
        outs = (shape(2 * TILE, 8 * TILE),)
        args = [meta, uv]
        if part == 1:
            outs = outs + (jax.ShapeDtypeStruct((groups, TILE, PACK), F32),)
            args = [*args, inverse, *profiles]
        return call(
            functools.partial(bands_kernel, part, n_row),
            outs,
            [SMEM] + [VMEM] * (len(args) - 1),
            [pltpu.VMEM((TILE, 8 * TILE), BF16)],
            name="bands",
            flops=4 * 10**9,
        )(*args)

    def blur(part, last, made, field, left, right, ends, other):
        ct, inv, *ready = made
        making = () if ready else (shape(TILE, 4 * TILE), shape(TILE, 8 * TILE), shape(2 * HALO, 2 * TILE))
        making = making if ct is not None else (shape(2 * TILE, 8 * TILE), *making)
        scratch = [pltpu.VMEM((4, 8 * TILE, TILE), BF16)]
        even = meta[4] % 2 == 0
        near = swap_pairs(jnp.where(even, ends[1], ends[0]), "row")
        far = lax.ppermute(jnp.where(even, ends[0], ends[1]), ("row", "col"), outer_rows(n_row, n_col))
        bot, top = jnp.where(even, near, far), jnp.where(even, far, near)
        rim = jax.ShapeDtypeStruct((depth, 2 * HALO, TILE), F32)
        outs = ((volume,) if part == 1 else ()) + (() if last else (narrow, strip, strip))
        main, *got = call(
            functools.partial(main_kernel, part, len(making) - 2 if making else 0),
            (rim,) + outs + making,
            [SMEM] + [VMEM] * 7,
            scratch if ct is not None else scratch + [pltpu.VMEM((TILE, 8 * TILE), BF16)],
            name="main",
            flops=4 * 10**9,
        )(meta, uv if ct is None else ct, uv if making else ready[1], field, left, right, other, inv)
        if making:
            got, ready = got[:-3], got[-3:]
        if ct is None:
            *got, ct = got
        cw, rt, edge = ready
        done = call(
            functools.partial(edge_kernel, part),
            outs,
            [SMEM] + [VMEM] * (7 + len(outs)),
            [pltpu.VMEM((PACK, 2 * TILE, TILE), BF16)],
            name="edge",
            flops=2 * 10**9,
        )(meta, cw, edge, main, top, bot, other, inv, *got)
        return done, (ct, inv, cw, rt, edge), near

    current = estimate
    others = [lax.ppermute(plane, "row", [(i, i ^ s) for i in range(n_row)]) for s in range(2, n_row)]
    forward = (None, jnp.zeros((groups, TILE, PACK), F32))
    backward = None
    for step in range(ITERS):
        last = step == ITERS - 1
        (ratio, *strips), forward, near = blur(0, False, forward, field, left, right, ends, observed)
        left, right = exchanged(*strips)
        if backward is None:
            backward = bands(1, lax.optimization_barrier((uv, strips[0]))[0], plane, near[-3:], *others)
        ends = ends_of(ratio, left, right)
        (current, *rest), backward, _ = blur(1, last, backward, ratio, left, right, ends, current)
        if not last:
            field, (left, right) = rest[0], exchanged(*rest[1:])
            ends = ends_of(field, left, right)
    return current


def solution(mesh):
    placed = (
        P(None, "row", "col"),
        P(None, "row", "col"),
        P(("row", "col"), None, None, None, None),
        P("row", "col", None, None),
        P("row", "col", None, None),
        P(None, "row", "col"),
    )
    return jax.shard_map(
        shards, mesh=mesh, in_specs=placed, out_specs=P(None, "row", "col"), check_vma=False
    )
```

```python
import functools

import jax
import jax.numpy as jnp
import numpy as np
from jax import lax
from jax.experimental import pallas as pl
from jax.experimental.pallas import tpu as pltpu
from jax.sharding import PartitionSpec as P

ITERS = 2
F32 = jnp.float32
BF16 = jnp.bfloat16
HIGHEST = lax.Precision.HIGHEST
VMEM = pl.BlockSpec(memory_space=pltpu.VMEM)
SMEM = pl.BlockSpec(memory_space=pltpu.SMEM)

TILE = 128
HALO = 16
PACK = TILE // HALO
TAP_ROWS = 48


def lanes(shape):
    return lax.broadcasted_iota(jnp.int32, shape, len(shape) - 1)


def sublanes(shape):
    return lax.broadcasted_iota(jnp.int32, shape, len(shape) - 2)


def call(body, outs, specs, scratch=(), name=None, flops=0, mib=16):
    return pl.pallas_call(
        body,
        out_shape=outs,
        in_specs=specs,
        out_specs=jax.tree.map(lambda _: VMEM, outs),
        scratch_shapes=list(scratch),
        compiler_params=pltpu.CompilerParams(vmem_limit_bytes=mib * 1024 * 1024),
        cost_estimate=pl.CostEstimate(flops=flops, bytes_accessed=1 << 20, transcendentals=0),
        name=name,
    )


def shift(cells, axis, by):
    count = lax.axis_size(axis)
    return lax.ppermute(cells, axis, [(i, (i + by) % count) for i in range(count)])


def swap(cells, axis, pairs):
    return lax.ppermute(cells, axis, pairs + [(j, i) for i, j in pairs])


def swap_pairs(cells, axis):
    return swap(cells, axis, [(i, i + 1) for i in range(0, lax.axis_size(axis), 2)])


def outer_columns(rows, cols):
    pairs = []
    for r in range(rows):
        for c in range(cols):
            to = c - 1 if c % 2 == 0 else c + 1
            pairs.append((r * cols + c, r * cols + to if 0 <= to < cols else (r ^ 1) * cols + c))
    return pairs


def outer_rows(rows, cols):
    pairs = []
    for r in range(rows):
        for c in range(cols):
            to = r - 1 if r % 2 == 0 else r + 1
            pairs.append((r * cols + c, to * cols + c if 0 <= to < rows else r * cols + (c ^ 1)))
    return pairs


def bank_kernel(bank_ref, out_ref):
    rows, taps = bank_ref.shape
    for block in range(rows // TILE):
        part = bank_ref[block * TILE : (block + 1) * TILE, :]
        part = jnp.concatenate([part, jnp.zeros((TILE, TILE - taps), F32)], axis=1)
        out_ref[:, block * TILE : (block + 1) * TILE] = part.T[:TAP_ROWS].astype(BF16)


def pick_kernel(cols, meta_ref, mine_ref, other_ref, *refs):
    pieces, outs = refs[:-2], refs[-2:]
    zones = pieces[0].shape[1] // TILE
    for keys_ref, out_ref in zip((mine_ref, other_ref), outs):
        ids = (keys_ref[...] + 0.5).astype(jnp.int32)
        for k in range(out_ref.shape[0]):
            got = jnp.zeros((TAP_ROWS, TILE), F32)
            for s, piece in enumerate(pieces):
                first = (meta_ref[5] ^ (2 * s)) * zones
                for m in range(zones):
                    got = jnp.where(
                        ids[k : k + 1] == first + m, piece[:, m * TILE : (m + 1) * TILE].astype(F32), got
                    )
            out_ref[k] = got.astype(BF16)


def taps_kernel(taps, keys_ref, mine_ref, other_ref, uv_ref):
    blended = mine_ref.shape[0]
    lane = lanes((1, TILE))
    is_row = (lane & 7) < 4
    picked = []
    total = jnp.zeros((1, TILE), F32)
    mix = keys_ref[blended:, :]
    for k in range(blended):
        got = mine_ref[k].astype(F32) + other_ref[k].astype(F32)
        sums = jnp.sum(got, axis=0, keepdims=True)
        both = sums * pltpu.roll(sums, TILE - 4, 1)
        total = total + jnp.where(is_row, both * mix[k : k + 1], 0.0)
        picked.append(got)
    group = (lanes((TILE, TILE)) >> 3) == (sublanes((TILE, TILE)) >> 3)
    total = jnp.dot(
        jnp.broadcast_to(total, (8, TILE)),
        group.astype(F32),
        precision=HIGHEST,
        preferred_element_type=F32,
    )[:1]
    tap = sublanes((TAP_ROWS, 2 * TILE))
    at = lanes((TAP_ROWS, 2 * TILE))
    half = taps // 2
    goes = jnp.where(at < TILE, (tap - half) & (TILE - 1), TILE + ((half - tap) & (TILE - 1)))
    place = ((goes == at) & (tap < taps)).astype(F32).astype(BF16)
    for k in range(blended):
        got = picked[k]
        scaled = mix[k : k + 1] * got / total
        chosen = jnp.where(is_row, scaled, got).astype(BF16)
        uv_ref[k] = lax.dot_general(
            chosen, place, (((0,), (0,)), ((), ())), preferred_element_type=F32
        ).reshape(uv_ref.shape[1:])


def turned(uv_ref, z, k, r, part, rows, by):
    line = uv_ref[k, z, r : r + 1, part * TILE : (part + 1) * TILE]
    return pltpu.roll(
        jnp.broadcast_to(line, (rows, TILE)), by % TILE, 1, stride=1, stride_axis=0
    )


def bands_kernel(part, rows, meta_ref, uv_ref, *refs):
    *refs, shifts_ref = refs
    if part == 0:
        (ct_ref,) = refs
    else:
        inverse_ref, illum, (ct_ref, inv_ref) = refs[0], refs[1 : 1 + rows], refs[1 + rows :]
        coarse = inverse_ref.shape[1] // rows
        smooth = jnp.zeros((TILE, illum[0].shape[1]), F32)
        for s in range(rows):
            first = pl.multiple_of((meta_ref[4] ^ s) * coarse, coarse)
            profile = sum(illum[s][n].astype(F32) for n in range(3))
            smooth = smooth + lax.dot_general(
                inverse_ref[meta_ref[4], pl.ds(first, coarse), :],
                profile.T[:coarse],
                (((0,), (0,)), ((), ())),
                precision=HIGHEST,
                preferred_element_type=F32,
            )
        inv = 1.0 / smooth
        for g in range(inv_ref.shape[0]):
            inv_ref[g] = inv[:, g * PACK : (g + 1) * PACK]
    start_shifts(shifts_ref)
    ct_ref[:, TILE:, :] = jnp.zeros((ct_ref.shape[0], TILE, 8 * TILE), BF16)

    def group(g8, carry):
        for i in range(PACK):
            column_bands(part, uv_ref, shifts_ref, g8 * PACK + i, i, ct_ref)
        return carry

    for g8 in range(ct_ref.shape[0] // PACK):
        group(g8, 0)


def start_shifts(shifts_ref):
    for t in range(PACK):
        to = (sublanes((TILE, TILE)) + t * HALO) & (TILE - 1)
        shifts_ref[:, t * TILE : (t + 1) * TILE] = (to == lanes((TILE, TILE))).astype(F32).astype(BF16)


def column_bands(part, uv_ref, shifts_ref, z, i, ct_ref):
    low_all = lanes((TILE, TILE)) < TILE // 2
    none = jnp.zeros((TILE, TILE), BF16)
    left, right = TILE + i * HALO, TILE + (i + 4) % PACK * HALO
    base = [turned(uv_ref, z, j // 4, 4 + j % 4, 1 - part, HALO, 0) for j in range(8)]
    base = jnp.concatenate(base, axis=0).astype(BF16)
    for t in range(0, PACK, 2):
        got = jnp.dot(
            base, shifts_ref[:, t * TILE : (t + 2) * TILE], preferred_element_type=F32
        ).astype(BF16)
        first, second = got[:, :TILE], got[:, TILE:]
        if t == 0:
            first, after = jnp.where(low_all, first, none), jnp.where(low_all, none, first)
        elif t == PACK - 2:
            second, before = jnp.where(low_all, none, second), jnp.where(low_all, second, none)
        for j in range(8):
            here, rows = slice(j * TILE, (j + 1) * TILE), slice(j * HALO, (j + 1) * HALO)
            ct_ref[z, t * HALO : (t + 1) * HALO, here] = first[rows]
            ct_ref[z, (t + 1) * HALO : (t + 2) * HALO, here] = second[rows]
            if t == 0:
                ct_ref[z, right : right + HALO, here] = after[rows]
            elif t == PACK - 2:
                ct_ref[z, left : left + HALO, here] = before[rows]


def other_bands(part, uv_ref, ct_ref, z, i, cw_ref, rt_ref, edge_ref):
    low = lanes((HALO, TILE)) < TILE // 2
    lane = lanes((HALO, TILE)) >> 4
    none = jnp.zeros((HALO, TILE), F32)
    above, below = [none] * 2, [none] * 2
    for j in range(8):
        here = slice(j * TILE, (j + 1) * TILE)
        full = turned(uv_ref, z, j // 4, j % 4, part, TILE, 0)
        first, last = full[:HALO], full[TILE - HALO :]
        rt_ref[z, :HALO, here] = jnp.where(low, first, none).astype(BF16)
        rt_ref[z, HALO : TILE - HALO, here] = full[HALO : TILE - HALO].astype(BF16)
        rt_ref[z, TILE - HALO :, here] = jnp.where(low, none, last).astype(BF16)
        spot = (j % 4) * 2
        above[j // 4] = jnp.where(lane == spot, full[(spot + 1) * HALO : (spot + 2) * HALO], above[j // 4])
        below[j // 4] = jnp.where(lane == spot + 1, full[spot * HALO : (spot + 1) * HALO], below[j // 4])
    edge_ref[z] = jnp.concatenate(
        [jnp.concatenate(above, axis=1), jnp.concatenate(below, axis=1)], axis=0
    ).astype(BF16)
    before, after = TILE + i * HALO, TILE + (i + 4) % PACK * HALO
    cw_ref[z, TILE - 2 * HALO :, :] = jnp.zeros((2 * HALO, 4 * TILE), BF16)
    for j in range(0, 8, 2):
        this, other = slice(j * TILE, (j + 1) * TILE), slice((j + 1) * TILE, (j + 2) * TILE)
        for t in range(6):
            a = before if t == 0 else (t - 1) * HALO
            b = after if t == 5 else (t + 3) * HALO
            cw_ref[z, t * HALO : (t + 1) * HALO, j * TILE // 2 : j * TILE // 2 + TILE] = jnp.where(
                low, ct_ref[z, a : a + HALO, this], ct_ref[z, b : b + HALO, other]
            )


def sides_of(left, right, meta_ref):
    left = jnp.where(meta_ref[0] > 0, left, jnp.zeros_like(left))
    right = jnp.where(meta_ref[1] > 0, right, jnp.zeros_like(right))
    return left, right


def joined(left, right, parity):
    low = lanes(left.shape) < TILE // 2
    return jnp.where(low, left, right) if parity == 0 else jnp.where(low, right, left)


def windows(field, left, right, i):
    lane = lanes(field.shape)
    left = pltpu.roll(left, -i * HALO % TILE, 1)
    right = pltpu.roll(right, (80 - (i + 4) % PACK * HALO) % TILE, 1)
    first = jnp.where(lane < HALO, left, pltpu.roll(field, HALO, 1))
    second = jnp.where(lane < 80, pltpu.roll(field, 80, 1), right)
    return first, second


def column_pass(wide, cw_ref, z, q_ref, slot):
    rows = wide.shape[0] // 2
    low = lanes((rows, TILE)) < TILE // 2
    for n in range(2):
        got = jnp.dot(
            wide, cw_ref[z, :, n * 256 : (n + 1) * 256], preferred_element_type=F32
        ).astype(BF16)
        for p in range(2):
            first, second = got[:rows, p * TILE : (p + 1) * TILE], got[rows:, p * TILE : (p + 1) * TILE]
            at = (n * 4 + p * 2) * rows
            q_ref[slot, at : at + rows, :] = jnp.where(low, first, pltpu.roll(second, TILE // 2, 1))
            q_ref[slot, at + rows : at + 2 * rows, :] = jnp.where(low, pltpu.roll(first, TILE // 2, 1), second)


def pack_strips(value, i, g8, rows, right_ref, left_ref):
    lane = lanes(value.shape) >> 4
    at = (i + 4) % PACK
    to_right = pltpu.roll(value, (i * HALO - 112) % TILE, 1)
    to_left = pltpu.roll(value, at * HALO, 1)
    if i == 0:
        right_ref[g8, rows] = to_right
        left_ref[g8, rows] = to_left
    else:
        right_ref[g8, rows] = jnp.where(lane == i, to_right, right_ref[g8, rows])
        left_ref[g8, rows] = jnp.where(lane == at, to_left, left_ref[g8, rows])


def finish(part, blurred, g8, i, rows, a_ref, inv_ref, outs):
    z = g8 * PACK + i
    if part == 0:
        value = a_ref[z, rows] / blurred
    else:
        value = a_ref[z, rows] * blurred * inv_ref[g8, rows, i : i + 1]
        outs[0][z, rows] = value
        outs = outs[1:]
    if outs:
        b_ref, right_ref, left_ref = outs
        value = value.astype(BF16)
        b_ref[z, rows] = value
        pack_strips(value, i, g8, rows, right_ref, left_ref)


def main_kernel(part, making, meta_ref, ct_ref, rt_ref, field_ref, left_ref, right_ref, a_ref, inv_ref, rim_ref, *refs):
    outs, q_ref = refs[:-1], refs[-1]
    if making:
        outs, made, uv_ref, rt_ref = outs[:-3], outs[-3:], rt_ref, outs[-2]
    if making == 2:
        shifts_ref, q_ref = refs[-1], refs[-2]
        *outs, ct_ref, cw_ref, rt_ref, edge_ref = refs[:-2]
        made = cw_ref, rt_ref, edge_ref
        start_shifts(shifts_ref)
        for z in range(ct_ref.shape[0]):
            for t in range(PACK):
                if t % 4 != z % 4:
                    ct_ref[z, TILE + t * HALO : TILE + (t + 1) * HALO, :] = jnp.zeros((HALO, 8 * TILE), BF16)
    inner = slice(HALO, TILE - HALO)

    def group(g8):
        sides = sides_of(left_ref[g8], right_ref[g8], meta_ref)
        halos = [joined(*sides, parity) for parity in range(2)]

        def columns(i):
            wide = jnp.concatenate([field_ref[g8 * PACK + i], halos[i // 4]], axis=1)
            for n in range(4):
                got = jnp.dot(
                    wide, ct_ref[g8 * PACK + i, :, n * 256 : (n + 1) * 256], preferred_element_type=F32
                ).astype(BF16)
                q_ref[i % 4, n * 256 : n * 256 + TILE, :] = got[:, :TILE]
                q_ref[i % 4, n * 256 + TILE : (n + 1) * 256, :] = got[:, TILE:]

        def rows(i):
            z = g8 * PACK + i
            blurred = jnp.dot(rt_ref[z], q_ref[i % 4], preferred_element_type=F32)
            rim_ref[z, :HALO] = blurred[:HALO]
            rim_ref[z, HALO:] = blurred[TILE - HALO :]
            finish(part, blurred[inner], g8, i, inner, a_ref, inv_ref, outs)

        def bands(i):
            if making == 2:
                column_bands(part, uv_ref, shifts_ref, g8 * PACK + i, i, ct_ref)
            if making:
                other_bands(part, uv_ref, ct_ref, g8 * PACK + i, i, *made)

        return bands, columns, rows

    count = field_ref.shape[0]
    steps = [group(g8) for g8 in range(count // PACK)]
    bands, columns, rows = ([(step[n], i) for step in steps for i in range(PACK)] for n in range(3))
    for z in range(-3, count):
        for kind, ahead in ((bands, 3), (columns, 2), (rows, 0)):
            if 0 <= z + ahead < count:
                do, i = kind[z + ahead]
                do(i)


def edge_kernel(part, meta_ref, cw_ref, edge_ref, rim_ref, top_ref, bot_ref, a_ref, inv_ref, *refs):
    count = len(refs) // 2
    made, outs, q_ref = refs[:count], refs[count:-1], refs[-1]
    depth = rim_ref.shape[0]
    inner = slice(HALO, TILE - HALO)

    def group(g8, carry):
        halos = [sides_of(ref[depth + g8], ref[depth + 2 + g8], meta_ref) for ref in (top_ref, bot_ref)]
        for old, new in zip(made, outs):
            each = pl.ds(g8 * (new.shape[0] // (depth // PACK)), new.shape[0] // (depth // PACK))
            new[each, inner] = old[each, inner]

        def columns(i):
            z = g8 * PACK + i
            pairs = []
            for s, ref in enumerate((top_ref, bot_ref)):
                both = windows(ref[z], *halos[s], i)
                pairs.append([jnp.where(meta_ref[2 + s] > 0, w, jnp.zeros_like(w)) for w in both])
            wide = jnp.concatenate([pairs[0][0], pairs[1][0], pairs[0][1], pairs[1][1]], axis=0)
            column_pass(wide, cw_ref, z, q_ref, i)

        def rows(i):
            z = g8 * PACK + i
            blurred = rim_ref[z] + jnp.dot(edge_ref[z], q_ref[i], preferred_element_type=F32)
            for s, at in enumerate((slice(0, HALO), slice(TILE - HALO, TILE))):
                finish(part, blurred[s * HALO : (s + 1) * HALO], g8, i, at, a_ref, inv_ref, outs)

        for i in range(PACK):
            columns(i)
        for i in range(PACK):
            rows(i)
        return carry

    for g8 in range(depth // PACK):
        group(g8, 0)


def keys_kernel(ids_ref, mix_ref, illum_ref, keys_ref, plane_ref):
    spread = (lanes((ids_ref.shape[1], TILE)) >> 3 == sublanes((ids_ref.shape[1], TILE))).astype(F32)
    both = jnp.concatenate([ids_ref[...].astype(F32), mix_ref[...]], axis=0)
    keys_ref[...] = jnp.dot(both, spread, precision=HIGHEST, preferred_element_type=F32)
    rest = illum_ref[:, 0, :]
    depth, coarse = rest.shape
    parts = []
    for _ in range(3):
        part = rest.astype(BF16)
        rest = rest - part.astype(F32)
        parts.append(jnp.concatenate([part, jnp.zeros((depth, TILE - coarse), BF16)], axis=1))
    for n in range(3):
        plane_ref[n] = parts[n]


def first_kernel(est_ref, b_ref, right_ref, left_ref):
    def group(g8, carry):
        for i in range(PACK):
            value = est_ref[g8 * PACK + i].astype(BF16)
            b_ref[g8 * PACK + i] = value
            pack_strips(value, i, g8, slice(0, TILE), right_ref, left_ref)
        return carry

    lax.fori_loop(0, est_ref.shape[0] // PACK, group, 0)


def smoothing(length, rows):
    stiffness = float(length * length) / 16.0
    d = np.diff(np.eye(length), axis=0)
    inverse = np.linalg.inv(np.eye(length) + stiffness * d.T @ d)
    wide = np.repeat(inverse, TILE * rows // length, axis=0)
    return jnp.asarray(wide.reshape(rows, TILE, length).transpose(0, 2, 1), F32)


def shards(observed, estimate, psf_bank, zone_ids, mix_weights, illumination):
    depth = estimate.shape[0]
    zones_here, _, _, rank, taps = psf_bank.shape
    n_row, n_col = lax.axis_size("row"), lax.axis_size("col")
    row, col = lax.axis_index("row"), lax.axis_index("col")
    groups = depth // PACK
    flag = lambda x: x.astype(jnp.int32)
    meta = jnp.stack(
        [flag(col > 0), flag(col < n_col - 1), flag(row > 0), flag(row < n_row - 1), flag(row), flag(col)]
    )
    volume = jax.ShapeDtypeStruct((depth, TILE, TILE), F32)
    narrow = jax.ShapeDtypeStruct((depth, TILE, TILE), BF16)
    strip = jax.ShapeDtypeStruct((groups, TILE, TILE), BF16)


    def ends_of(field, left, right, *more):
        return [
            jnp.concatenate([field[:, rows], left[:, rows], right[:, rows], *more], axis=0)
            for rows in (slice(0, HALO), slice(TILE - HALO, TILE))
        ]

    def exchanged(to_right, to_left):
        even = meta[5] % 2 == 0
        far = lax.ppermute(jnp.where(even, to_left, to_right), ("row", "col"), outer_columns(n_row, n_col))
        near = swap_pairs(jnp.where(even, to_right, to_left), "col")
        return jnp.where(even, far, near), jnp.where(even, near, far)

    blended = zone_ids.shape[-1]
    flat = (zones_here * depth * 2 * rank, taps)
    bank = call(
        bank_kernel,
        jax.ShapeDtypeStruct((TAP_ROWS, zones_here * TILE), BF16),
        [VMEM],
        name="bank",
        flops=4 * 10**9,
    )(psf_bank.reshape(flat))
    pieces = [bank] + [lax.ppermute(bank, "col", [(i, i ^ s) for i in range(n_col)]) for s in range(2, n_col, 2)]
    field, to_right, to_left = call(
        first_kernel, (narrow, strip, strip), [VMEM], name="first", flops=10**9
    )(estimate)
    keys, plane = call(
        keys_kernel,
        (jax.ShapeDtypeStruct((2 * blended, TILE), F32), jax.ShapeDtypeStruct((3, depth, TILE), BF16)),
        [VMEM] * 3,
        name="keys",
    )(zone_ids[0, 0].T, mix_weights[0, 0].T, illumination.transpose(0, 2, 1))
    other_keys = swap_pairs(keys, "col")
    left, right = exchanged(to_right, to_left)
    inverse = smoothing(illumination.shape[1] * n_row, n_row)
    factors = jax.ShapeDtypeStruct((blended, TAP_ROWS, TILE), BF16)
    mine, others = call(
        functools.partial(pick_kernel, n_col),
        (factors, factors),
        [SMEM] + [VMEM] * (2 + len(pieces)),
        name="pick",
    )(meta, keys, other_keys, *pieces)
    ends = ends_of(field, left, right, plane)
    uv = call(
        functools.partial(taps_kernel, taps),
        jax.ShapeDtypeStruct((blended, depth, 2 * rank, 2 * TILE), F32),
        [VMEM] * 3,
        name="taps",
    )(keys, mine, swap_pairs(others, "col"))

    shape = lambda *s: jax.ShapeDtypeStruct((depth,) + s, BF16)

    def bands(part, uv, *profiles):
        outs = (shape(2 * TILE, 8 * TILE),)
        args = [meta, uv]
        if part == 1:
            outs = outs + (jax.ShapeDtypeStruct((groups, TILE, PACK), F32),)
            args = [*args, inverse, *profiles]
        return call(
            functools.partial(bands_kernel, part, n_row),
            outs,
            [SMEM] + [VMEM] * (len(args) - 1),
            [pltpu.VMEM((TILE, 8 * TILE), BF16)],
            name="bands",
            flops=4 * 10**9,
        )(*args)

    def blur(part, last, made, field, left, right, ends, other):
        ct, inv, *ready = made
        making = () if ready else (shape(TILE, 4 * TILE), shape(TILE, 8 * TILE), shape(2 * HALO, 2 * TILE))
        making = making if ct is not None else (shape(2 * TILE, 8 * TILE), *making)
        scratch = [pltpu.VMEM((4, 8 * TILE, TILE), BF16)]
        even = meta[4] % 2 == 0
        far = lax.ppermute(jnp.where(even, ends[0], ends[1]), ("row", "col"), outer_rows(n_row, n_col))
        near = swap_pairs(jnp.where(even, ends[1], ends[0]), "row")
        bot, top = jnp.where(even, near, far), jnp.where(even, far, near)
        rim = jax.ShapeDtypeStruct((depth, 2 * HALO, TILE), F32)
        outs = ((volume,) if part == 1 else ()) + (() if last else (narrow, strip, strip))
        main, *got = call(
            functools.partial(main_kernel, part, len(making) - 2 if making else 0),
            (rim,) + outs + making,
            [SMEM] + [VMEM] * 7,
            scratch if ct is not None else scratch + [pltpu.VMEM((TILE, 8 * TILE), BF16)],
            name="main",
            flops=4 * 10**9,
        )(meta, uv if ct is None else ct, uv if making else ready[1], field, left, right, other, inv)
        if making:
            got, ready = got[:-3], got[-3:]
        if ct is None:
            *got, ct = got
        cw, rt, edge = ready
        done = call(
            functools.partial(edge_kernel, part),
            outs,
            [SMEM] + [VMEM] * (7 + len(outs)),
            [pltpu.VMEM((PACK, 2 * TILE, TILE), BF16)],
            name="edge",
            flops=2 * 10**9,
        )(meta, cw, edge, main, top, bot, other, inv, *got)
        return done, (ct, inv, cw, rt, edge), near

    current = estimate
    others = [lax.ppermute(plane, "row", [(i, i ^ s) for i in range(n_row)]) for s in range(2, n_row)]
    forward = (None, jnp.zeros((groups, TILE, PACK), F32))
    backward = None
    for step in range(ITERS):
        last = step == ITERS - 1
        (ratio, *strips), forward, near = blur(0, False, forward, field, left, right, ends, observed)
        left, right = exchanged(*strips)
        if backward is None:
            backward = bands(1, lax.optimization_barrier((uv, strips[0]))[0], plane, near[-3:], *others)
        ends = ends_of(ratio, left, right)
        (current, *rest), backward, _ = blur(1, last, backward, ratio, left, right, ends, current)
        if not last:
            field, (left, right) = rest[0], exchanged(*rest[1:])
            ends = ends_of(field, left, right)
    return current


def solution(mesh):
    placed = (
        P(None, "row", "col"),
        P(None, "row", "col"),
        P(("row", "col"), None, None, None, None),
        P("row", "col", None, None),
        P("row", "col", None, None),
        P(None, "row", "col"),
    )
    return jax.shard_map(
        shards, mesh=mesh, in_specs=placed, out_specs=P(None, "row", "col"), check_vma=False
    )
```

```python
import functools

import jax
import jax.numpy as jnp
import numpy as np
from jax import lax
from jax.experimental import pallas as pl
from jax.experimental.pallas import tpu as pltpu
from jax.sharding import PartitionSpec as P

ITERS = 2
F32 = jnp.float32
BF16 = jnp.bfloat16
HIGHEST = lax.Precision.HIGHEST
VMEM = pl.BlockSpec(memory_space=pltpu.VMEM)
SMEM = pl.BlockSpec(memory_space=pltpu.SMEM)

TILE = 128
HALO = 16
PACK = TILE // HALO
TAP_ROWS = 48


def lanes(shape):
    return lax.broadcasted_iota(jnp.int32, shape, len(shape) - 1)


def sublanes(shape):
    return lax.broadcasted_iota(jnp.int32, shape, len(shape) - 2)


def call(body, outs, specs, scratch=(), name=None, flops=0, to=VMEM):
    return pl.pallas_call(
        body,
        out_shape=outs,
        in_specs=specs,
        out_specs=jax.tree.map(lambda _: to, outs),
        scratch_shapes=list(scratch),
        compiler_params=pltpu.CompilerParams(vmem_limit_bytes=16 * 1024 * 1024),
        cost_estimate=pl.CostEstimate(flops=flops, bytes_accessed=1 << 20, transcendentals=0),
        name=name,
    )


def shift(cells, axis, by):
    count = lax.axis_size(axis)
    return lax.ppermute(cells, axis, [(i, (i + by) % count) for i in range(count)])


def swap(cells, axis, pairs):
    return lax.ppermute(cells, axis, pairs + [(j, i) for i, j in pairs])


def swap_pairs(cells, axis):
    return swap(cells, axis, [(i, i + 1) for i in range(0, lax.axis_size(axis), 2)])


def outer_columns(rows, cols):
    pairs = []
    for r in range(rows):
        for c in range(cols):
            to = c - 1 if c % 2 == 0 else c + 1
            pairs.append((r * cols + c, r * cols + to if 0 <= to < cols else (r ^ 1) * cols + c))
    return pairs


def outer_rows(rows, cols):
    pairs = []
    for r in range(rows):
        for c in range(cols):
            to = r - 1 if r % 2 == 0 else r + 1
            pairs.append((r * cols + c, to * cols + c if 0 <= to < rows else r * cols + (c ^ 1)))
    return pairs


def bank_kernel(bank_ref, out_ref):
    rows, taps = bank_ref.shape
    for block in range(rows // TILE):
        part = bank_ref[block * TILE : (block + 1) * TILE, :]
        part = jnp.concatenate([part, jnp.zeros((TILE, TILE - taps), F32)], axis=1)
        out_ref[:, block * TILE : (block + 1) * TILE] = part.T[:TAP_ROWS].astype(BF16)


def pick_kernel(cols, meta_ref, mine_ref, other_ref, *refs):
    pieces, outs = refs[:-2], refs[-2:]
    zones = pieces[0].shape[1] // TILE
    for keys_ref, out_ref in zip((mine_ref, other_ref), outs):
        ids = (keys_ref[...] + 0.5).astype(jnp.int32)
        for k in range(out_ref.shape[0]):
            got = jnp.zeros((TAP_ROWS, TILE), F32)
            for s, piece in enumerate(pieces):
                first = (meta_ref[5] ^ (2 * s)) * zones
                for m in range(zones):
                    got = jnp.where(
                        ids[k : k + 1] == first + m, piece[:, m * TILE : (m + 1) * TILE].astype(F32), got
                    )
            out_ref[k] = got.astype(BF16)


def taps_kernel(taps, keys_ref, mine_ref, other_ref, uv_ref):
    blended = mine_ref.shape[0]
    lane = lanes((1, TILE))
    is_row = (lane & 7) < 4
    picked = []
    total = jnp.zeros((1, TILE), F32)
    mix = keys_ref[blended:, :]
    for k in range(blended):
        got = mine_ref[k].astype(F32) + other_ref[k].astype(F32)
        sums = jnp.sum(got, axis=0, keepdims=True)
        both = sums * pltpu.roll(sums, TILE - 4, 1)
        total = total + jnp.where(is_row, both * mix[k : k + 1], 0.0)
        picked.append(got)
    group = (lanes((TILE, TILE)) >> 3) == (sublanes((TILE, TILE)) >> 3)
    total = jnp.dot(
        jnp.broadcast_to(total, (8, TILE)),
        group.astype(F32),
        precision=HIGHEST,
        preferred_element_type=F32,
    )[:1]
    tap = sublanes((TAP_ROWS, 2 * TILE))
    at = lanes((TAP_ROWS, 2 * TILE))
    half = taps // 2
    goes = jnp.where(at < TILE, (tap - half) & (TILE - 1), TILE + ((half - tap) & (TILE - 1)))
    place = ((goes == at) & (tap < taps)).astype(F32).astype(BF16)
    for k in range(blended):
        got = picked[k]
        scaled = mix[k : k + 1] * got / total
        chosen = jnp.where(is_row, scaled, got).astype(BF16)
        uv_ref[k] = lax.dot_general(
            chosen, place, (((0,), (0,)), ((), ())), preferred_element_type=F32
        ).reshape(uv_ref.shape[1:])


def turned(uv_ref, z, k, r, part, rows, by):
    line = uv_ref[k, z, r : r + 1, part * TILE : (part + 1) * TILE]
    return pltpu.roll(
        jnp.broadcast_to(line, (rows, TILE)), by % TILE, 1, stride=1, stride_axis=0
    )


def bands_kernel(part, rows, meta_ref, uv_ref, *refs):
    *refs, shifts_ref = refs
    if part == 0:
        (ct_ref,) = refs
    else:
        inverse_ref, illum, (ct_ref, inv_ref) = refs[0], refs[1 : 1 + rows], refs[1 + rows :]
        coarse = inverse_ref.shape[1] // rows
        smooth = jnp.zeros((TILE, illum[0].shape[1]), F32)
        for s in range(rows):
            first = pl.multiple_of((meta_ref[4] ^ s) * coarse, coarse)
            profile = sum(illum[s][n].astype(F32) for n in range(3))
            smooth = smooth + lax.dot_general(
                inverse_ref[meta_ref[4], pl.ds(first, coarse), :],
                profile.T[:coarse],
                (((0,), (0,)), ((), ())),
                precision=HIGHEST,
                preferred_element_type=F32,
            )
        inv = 1.0 / smooth
        for g in range(inv_ref.shape[0]):
            inv_ref[g] = inv[:, g * PACK : (g + 1) * PACK]
    start_shifts(shifts_ref)
    ct_ref[:, TILE:, :] = jnp.zeros((ct_ref.shape[0], TILE, 8 * TILE), BF16)

    def group(g8, carry):
        for i in range(PACK):
            column_bands(part, uv_ref, shifts_ref, g8 * PACK + i, i, ct_ref)
        return carry

    for g8 in range(ct_ref.shape[0] // PACK):
        group(g8, 0)


def start_shifts(shifts_ref):
    for t in range(PACK):
        to = (sublanes((TILE, TILE)) + t * HALO) & (TILE - 1)
        shifts_ref[:, t * TILE : (t + 1) * TILE] = (to == lanes((TILE, TILE))).astype(F32).astype(BF16)


def column_bands(part, uv_ref, shifts_ref, z, i, ct_ref):
    low_all = lanes((TILE, TILE)) < TILE // 2
    none = jnp.zeros((TILE, TILE), BF16)
    left, right = TILE + i * HALO, TILE + (i + 4) % PACK * HALO
    base = [turned(uv_ref, z, j // 4, 4 + j % 4, 1 - part, HALO, 0) for j in range(8)]
    base = jnp.concatenate(base, axis=0).astype(BF16)
    for t in range(0, PACK, 2):
        got = jnp.dot(
            base, shifts_ref[:, t * TILE : (t + 2) * TILE], preferred_element_type=F32
        ).astype(BF16)
        first, second = got[:, :TILE], got[:, TILE:]
        if t == 0:
            first, after = jnp.where(low_all, first, none), jnp.where(low_all, none, first)
        elif t == PACK - 2:
            second, before = jnp.where(low_all, none, second), jnp.where(low_all, second, none)
        for j in range(8):
            here, rows = slice(j * TILE, (j + 1) * TILE), slice(j * HALO, (j + 1) * HALO)
            ct_ref[z, t * HALO : (t + 1) * HALO, here] = first[rows]
            ct_ref[z, (t + 1) * HALO : (t + 2) * HALO, here] = second[rows]
            if t == 0:
                ct_ref[z, right : right + HALO, here] = after[rows]
            elif t == PACK - 2:
                ct_ref[z, left : left + HALO, here] = before[rows]


def other_bands(part, uv_ref, ct_ref, z, i, cw_ref, rt_ref, edge_ref):
    low = lanes((HALO, TILE)) < TILE // 2
    lane = lanes((HALO, TILE)) >> 4
    none = jnp.zeros((HALO, TILE), F32)
    above, below = [none] * 2, [none] * 2
    for j in range(8):
        here = slice(j * TILE, (j + 1) * TILE)
        full = turned(uv_ref, z, j // 4, j % 4, part, TILE, 0)
        first, last = full[:HALO], full[TILE - HALO :]
        rt_ref[z, :HALO, here] = jnp.where(low, first, none).astype(BF16)
        rt_ref[z, HALO : TILE - HALO, here] = full[HALO : TILE - HALO].astype(BF16)
        rt_ref[z, TILE - HALO :, here] = jnp.where(low, none, last).astype(BF16)
        spot = (j % 4) * 2
        above[j // 4] = jnp.where(lane == spot, full[(spot + 1) * HALO : (spot + 2) * HALO], above[j // 4])
        below[j // 4] = jnp.where(lane == spot + 1, full[spot * HALO : (spot + 1) * HALO], below[j // 4])
    edge_ref[z] = jnp.concatenate(
        [jnp.concatenate(above, axis=1), jnp.concatenate(below, axis=1)], axis=0
    ).astype(BF16)
    before, after = TILE + i * HALO, TILE + (i + 4) % PACK * HALO
    cw_ref[z, TILE - 2 * HALO :, :] = jnp.zeros((2 * HALO, 4 * TILE), BF16)
    for j in range(0, 8, 2):
        this, other = slice(j * TILE, (j + 1) * TILE), slice((j + 1) * TILE, (j + 2) * TILE)
        for t in range(6):
            a = before if t == 0 else (t - 1) * HALO
            b = after if t == 5 else (t + 3) * HALO
            cw_ref[z, t * HALO : (t + 1) * HALO, j * TILE // 2 : j * TILE // 2 + TILE] = jnp.where(
                low, ct_ref[z, a : a + HALO, this], ct_ref[z, b : b + HALO, other]
            )


def sides_of(left, right, meta_ref):
    left = jnp.where(meta_ref[0] > 0, left, jnp.zeros_like(left))
    right = jnp.where(meta_ref[1] > 0, right, jnp.zeros_like(right))
    return left, right


def joined(left, right, parity):
    low = lanes(left.shape) < TILE // 2
    return jnp.where(low, left, right) if parity == 0 else jnp.where(low, right, left)


def windows(field, left, right, i):
    lane = lanes(field.shape)
    left = pltpu.roll(left, -i * HALO % TILE, 1)
    right = pltpu.roll(right, (80 - (i + 4) % PACK * HALO) % TILE, 1)
    first = jnp.where(lane < HALO, left, pltpu.roll(field, HALO, 1))
    second = jnp.where(lane < 80, pltpu.roll(field, 80, 1), right)
    return first, second


def column_pass(wide, cw_ref, z, q_ref, slot):
    rows = wide.shape[0] // 2
    low = lanes((rows, TILE)) < TILE // 2
    for n in range(2):
        got = jnp.dot(
            wide, cw_ref[z, :, n * 256 : (n + 1) * 256], preferred_element_type=F32
        ).astype(BF16)
        for p in range(2):
            first, second = got[:rows, p * TILE : (p + 1) * TILE], got[rows:, p * TILE : (p + 1) * TILE]
            at = (n * 4 + p * 2) * rows
            q_ref[slot, at : at + rows, :] = jnp.where(low, first, pltpu.roll(second, TILE // 2, 1))
            q_ref[slot, at + rows : at + 2 * rows, :] = jnp.where(low, pltpu.roll(first, TILE // 2, 1), second)


def pack_strips(value, i, g8, rows, right_ref, left_ref):
    lane = lanes(value.shape) >> 4
    at = (i + 4) % PACK
    to_right = pltpu.roll(value, (i * HALO - 112) % TILE, 1)
    to_left = pltpu.roll(value, at * HALO, 1)
    if i == 0:
        right_ref[g8, rows] = to_right
        left_ref[g8, rows] = to_left
    else:
        right_ref[g8, rows] = jnp.where(lane == i, to_right, right_ref[g8, rows])
        left_ref[g8, rows] = jnp.where(lane == at, to_left, left_ref[g8, rows])


def finish(part, blurred, g8, i, rows, a_ref, inv_ref, outs):
    z = g8 * PACK + i
    if part == 0:
        value = a_ref[z, rows] / blurred
    else:
        value = a_ref[z, rows] * blurred * inv_ref[g8, rows, i : i + 1]
        outs[0][z, rows] = value
        outs = outs[1:]
    if outs:
        b_ref, right_ref, left_ref = outs
        value = value.astype(BF16)
        b_ref[z, rows] = value
        pack_strips(value, i, g8, rows, right_ref, left_ref)


def main_kernel(part, making, meta_ref, ct_ref, rt_ref, field_ref, left_ref, right_ref, a_ref, inv_ref, rim_ref, *refs):
    outs, q_ref = refs[:-1], refs[-1]
    if making:
        outs, made, uv_ref, rt_ref = outs[:-3], outs[-3:], rt_ref, outs[-2]
    if making == 2:
        shifts_ref, q_ref = refs[-1], refs[-2]
        *outs, ct_ref, cw_ref, rt_ref, edge_ref = refs[:-2]
        made = cw_ref, rt_ref, edge_ref
        start_shifts(shifts_ref)
        for z in range(ct_ref.shape[0]):
            for t in range(PACK):
                if t % 4 != z % 4:
                    ct_ref[z, TILE + t * HALO : TILE + (t + 1) * HALO, :] = jnp.zeros((HALO, 8 * TILE), BF16)
    inner = slice(HALO, TILE - HALO)

    def group(g8):
        sides = sides_of(left_ref[g8], right_ref[g8], meta_ref)
        halos = [joined(*sides, parity) for parity in range(2)]

        def columns(i):
            wide = jnp.concatenate([field_ref[g8 * PACK + i], halos[i // 4]], axis=1)
            for n in range(4):
                got = jnp.dot(
                    wide, ct_ref[g8 * PACK + i, :, n * 256 : (n + 1) * 256], preferred_element_type=F32
                ).astype(BF16)
                q_ref[i % 4, n * 256 : n * 256 + TILE, :] = got[:, :TILE]
                q_ref[i % 4, n * 256 + TILE : (n + 1) * 256, :] = got[:, TILE:]

        def rows(i):
            z = g8 * PACK + i
            blurred = jnp.dot(rt_ref[z], q_ref[i % 4], preferred_element_type=F32)
            rim_ref[z, :HALO] = blurred[:HALO]
            rim_ref[z, HALO:] = blurred[TILE - HALO :]
            finish(part, blurred[inner], g8, i, inner, a_ref, inv_ref, outs)

        def bands(i):
            if making == 2:
                column_bands(part, uv_ref, shifts_ref, g8 * PACK + i, i, ct_ref)
            if making:
                other_bands(part, uv_ref, ct_ref, g8 * PACK + i, i, *made)

        return bands, columns, rows

    count = field_ref.shape[0]
    steps = [group(g8) for g8 in range(count // PACK)]
    bands, columns, rows = ([(step[n], i) for step in steps for i in range(PACK)] for n in range(3))
    for z in range(-3, count):
        for kind, ahead in ((bands, 3), (columns, 2), (rows, 0)):
            if 0 <= z + ahead < count:
                do, i = kind[z + ahead]
                do(i)


def edge_kernel(part, last, meta_ref, cw_ref, edge_ref, rim_ref, top_ref, bot_ref, a_ref, inv_ref, *refs):
    if last:
        made, (result, q_ref, whole, sems) = refs[:1], refs[1:]
        outs = (whole,)
    else:
        count = len(refs) // 2
        made, outs, q_ref = refs[:count], refs[count:-1], refs[-1]
    copies = []
    depth = rim_ref.shape[0]
    inner = slice(HALO, TILE - HALO)

    def group(g8, carry):
        halos = [sides_of(ref[depth + g8], ref[depth + 2 + g8], meta_ref) for ref in (top_ref, bot_ref)]
        for old, new in zip(made, outs):
            each = pl.ds(g8 * (new.shape[0] // (depth // PACK)), new.shape[0] // (depth // PACK))
            new[each, inner] = old[each, inner]

        def columns(i):
            z = g8 * PACK + i
            pairs = []
            for s, ref in enumerate((top_ref, bot_ref)):
                both = windows(ref[z], *halos[s], i)
                pairs.append([jnp.where(meta_ref[2 + s] > 0, w, jnp.zeros_like(w)) for w in both])
            wide = jnp.concatenate([pairs[0][0], pairs[1][0], pairs[0][1], pairs[1][1]], axis=0)
            column_pass(wide, cw_ref, z, q_ref, i)

        def rows(i):
            z = g8 * PACK + i
            blurred = rim_ref[z] + jnp.dot(edge_ref[z], q_ref[i], preferred_element_type=F32)
            for s, at in enumerate((slice(0, HALO), slice(TILE - HALO, TILE))):
                finish(part, blurred[s * HALO : (s + 1) * HALO], g8, i, at, a_ref, inv_ref, outs)

        for i in range(PACK):
            columns(i)
        for i in range(PACK):
            rows(i)
            if last and i % 4 == 3:
                ready = pl.ds(g8 * PACK + i - 3, 4)
                copies.append(pltpu.make_async_copy(whole.at[ready], result.at[ready], sems.at[len(copies)]))
                copies[-1].start()
        return carry

    for g8 in range(depth // PACK):
        group(g8, 0)
    for copy in copies:
        copy.wait()


def keys_kernel(ids_ref, mix_ref, illum_ref, keys_ref, plane_ref):
    spread = (lanes((ids_ref.shape[1], TILE)) >> 3 == sublanes((ids_ref.shape[1], TILE))).astype(F32)
    both = jnp.concatenate([ids_ref[...].astype(F32), mix_ref[...]], axis=0)
    keys_ref[...] = jnp.dot(both, spread, precision=HIGHEST, preferred_element_type=F32)
    rest = illum_ref[:, 0, :]
    depth, coarse = rest.shape
    parts = []
    for _ in range(3):
        part = rest.astype(BF16)
        rest = rest - part.astype(F32)
        parts.append(jnp.concatenate([part, jnp.zeros((depth, TILE - coarse), BF16)], axis=1))
    for n in range(3):
        plane_ref[n] = parts[n]


def first_kernel(est_ref, b_ref, right_ref, left_ref):
    def group(g8, carry):
        for i in range(PACK):
            value = est_ref[g8 * PACK + i].astype(BF16)
            b_ref[g8 * PACK + i] = value
            pack_strips(value, i, g8, slice(0, TILE), right_ref, left_ref)
        return carry

    lax.fori_loop(0, est_ref.shape[0] // PACK, group, 0)


def smoothing(length, rows):
    stiffness = float(length * length) / 16.0
    d = np.diff(np.eye(length), axis=0)
    inverse = np.linalg.inv(np.eye(length) + stiffness * d.T @ d)
    wide = np.repeat(inverse, TILE * rows // length, axis=0)
    return jnp.asarray(wide.reshape(rows, TILE, length).transpose(0, 2, 1), F32)


def shards(observed, estimate, psf_bank, zone_ids, mix_weights, illumination):
    depth = estimate.shape[0]
    zones_here, _, _, rank, taps = psf_bank.shape
    n_row, n_col = lax.axis_size("row"), lax.axis_size("col")
    row, col = lax.axis_index("row"), lax.axis_index("col")
    groups = depth // PACK
    flag = lambda x: x.astype(jnp.int32)
    meta = jnp.stack(
        [flag(col > 0), flag(col < n_col - 1), flag(row > 0), flag(row < n_row - 1), flag(row), flag(col)]
    )
    volume = jax.ShapeDtypeStruct((depth, TILE, TILE), F32)
    narrow = jax.ShapeDtypeStruct((depth, TILE, TILE), BF16)
    strip = jax.ShapeDtypeStruct((groups, TILE, TILE), BF16)


    def ends_of(field, left, right, *more):
        return [
            jnp.concatenate([field[:, rows], left[:, rows], right[:, rows], *more], axis=0)
            for rows in (slice(0, HALO), slice(TILE - HALO, TILE))
        ]

    def exchanged(to_right, to_left):
        even = meta[5] % 2 == 0
        far = lax.ppermute(jnp.where(even, to_left, to_right), ("row", "col"), outer_columns(n_row, n_col))
        near = swap_pairs(jnp.where(even, to_right, to_left), "col")
        return jnp.where(even, far, near), jnp.where(even, near, far)

    blended = zone_ids.shape[-1]
    flat = (zones_here * depth * 2 * rank, taps)
    bank = call(
        bank_kernel,
        jax.ShapeDtypeStruct((TAP_ROWS, zones_here * TILE), BF16),
        [VMEM],
        name="bank",
        flops=4 * 10**9,
    )(psf_bank.reshape(flat))
    pieces = [bank] + [lax.ppermute(bank, "col", [(i, i ^ s) for i in range(n_col)]) for s in range(2, n_col, 2)]
    field, to_right, to_left = call(
        first_kernel, (narrow, strip, strip), [VMEM], name="first", flops=10**9
    )(estimate)
    keys, plane = call(
        keys_kernel,
        (jax.ShapeDtypeStruct((2 * blended, TILE), F32), jax.ShapeDtypeStruct((3, depth, TILE), BF16)),
        [VMEM] * 3,
        name="keys",
    )(zone_ids[0, 0].T, mix_weights[0, 0].T, illumination.transpose(0, 2, 1))
    other_keys = swap_pairs(keys, "col")
    left, right = exchanged(to_right, to_left)
    inverse = smoothing(illumination.shape[1] * n_row, n_row)
    factors = jax.ShapeDtypeStruct((blended, TAP_ROWS, TILE), BF16)
    mine, others = call(
        functools.partial(pick_kernel, n_col),
        (factors, factors),
        [SMEM] + [VMEM] * (2 + len(pieces)),
        name="pick",
    )(meta, keys, other_keys, *pieces)
    ends = ends_of(field, left, right, plane)
    uv = call(
        functools.partial(taps_kernel, taps),
        jax.ShapeDtypeStruct((blended, depth, 2 * rank, 2 * TILE), F32),
        [VMEM] * 3,
        name="taps",
    )(keys, mine, swap_pairs(others, "col"))

    shape = lambda *s: jax.ShapeDtypeStruct((depth,) + s, BF16)

    def bands(part, uv, *profiles):
        outs = (shape(2 * TILE, 8 * TILE),)
        args = [meta, uv]
        if part == 1:
            outs = outs + (jax.ShapeDtypeStruct((groups, TILE, PACK), F32),)
            args = [*args, inverse, *profiles]
        return call(
            functools.partial(bands_kernel, part, n_row),
            outs,
            [SMEM] + [VMEM] * (len(args) - 1),
            [pltpu.VMEM((TILE, 8 * TILE), BF16)],
            name="bands",
            flops=4 * 10**9,
        )(*args)

    def blur(part, last, made, field, left, right, ends, other):
        ct, inv, *ready = made
        making = () if ready else (shape(TILE, 4 * TILE), shape(TILE, 8 * TILE), shape(2 * HALO, 2 * TILE))
        making = making if ct is not None else (shape(2 * TILE, 8 * TILE), *making)
        scratch = [pltpu.VMEM((4, 8 * TILE, TILE), BF16)]
        even = meta[4] % 2 == 0
        far = lax.ppermute(jnp.where(even, ends[0], ends[1]), ("row", "col"), outer_rows(n_row, n_col))
        near = swap_pairs(jnp.where(even, ends[1], ends[0]), "row")
        bot, top = jnp.where(even, near, far), jnp.where(even, far, near)
        rim = jax.ShapeDtypeStruct((depth, 2 * HALO, TILE), F32)
        outs = ((volume,) if part == 1 else ()) + (() if last else (narrow, strip, strip))
        main, *got = call(
            functools.partial(main_kernel, part, len(making) - 2 if making else 0),
            (rim,) + outs + making,
            [SMEM] + [VMEM] * 7,
            scratch if ct is not None else scratch + [pltpu.VMEM((TILE, 8 * TILE), BF16)],
            name="main",
            flops=4 * 10**9,
        )(meta, uv if ct is None else ct, uv if making else ready[1], field, left, right, other, inv)
        if making:
            got, ready = got[:-3], got[-3:]
        if ct is None:
            *got, ct = got
        cw, rt, edge = ready
        leaving = [pltpu.VMEM(volume.shape, F32), pltpu.SemaphoreType.DMA((depth // 4,))] if last else []
        done = call(
            functools.partial(edge_kernel, part, last),
            outs,
            [SMEM] + [VMEM] * (7 + len(outs)),
            [pltpu.VMEM((PACK, 2 * TILE, TILE), BF16), *leaving],
            to=pl.BlockSpec(memory_space=pl.ANY) if last else VMEM,
            name="edge",
            flops=2 * 10**9,
        )(meta, cw, edge, main, top, bot, other, inv, *got)
        return done, (ct, inv, cw, rt, edge), near

    current = estimate
    others = [lax.ppermute(plane, "row", [(i, i ^ s) for i in range(n_row)]) for s in range(2, n_row)]
    forward = (None, jnp.zeros((groups, TILE, PACK), F32))
    backward = None
    for step in range(ITERS):
        last = step == ITERS - 1
        (ratio, *strips), forward, near = blur(0, False, forward, field, left, right, ends, observed)
        left, right = exchanged(*strips)
        if backward is None:
            backward = bands(1, lax.optimization_barrier((uv, strips[0]))[0], plane, near[-3:], *others)
        ends = ends_of(ratio, left, right)
        (current, *rest), backward, _ = blur(1, last, backward, ratio, left, right, ends, current)
        if not last:
            field, (left, right) = rest[0], exchanged(*rest[1:])
            ends = ends_of(field, left, right)
    return current


def solution(mesh):
    placed = (
        P(None, "row", "col"),
        P(None, "row", "col"),
        P(("row", "col"), None, None, None, None),
        P("row", "col", None, None),
        P("row", "col", None, None),
        P(None, "row", "col"),
    )
    return jax.shard_map(
        shards, mesh=mesh, in_specs=placed, out_specs=P(None, "row", "col"), check_vma=False
    )
```
